256 devices in a mesh: grp: 16 (over x_lo, z), sp: 16 (over y, x_hi, core).
Axes of the slice: x: 4 (x_hi: 2, x_lo: 2; x = x_hi * 2 + x_lo), y: 4, z: 8, core: 2. Of those that a mesh axis runs over, the one named last changes fastest.
Arguments:
- query: bfloat16 [32768, 6144], P(('grp', 'sp')), may hold values from -160 to 160
- key: bfloat16 [32768, 512], P(('grp', 'sp')), may hold values from -160 to 160
- value: bfloat16 [32768, 512], P(('grp', 'sp')), may hold values from -6 to 6
- grad_out: bfloat16 [32768, 6144], P(('grp', 'sp')), may hold values from -64 to 64
- segment_ids: int32 [32768], P(('grp', 'sp')), may hold values from 0 to 63, never falling along the last dimension, each value on 1 to 2048 neighbouring positions
Outputs:
- grad_query: bfloat16 [32768, 6144], P(('grp', 'sp'))
- grad_key: bfloat16 [32768, 512], P(('grp', 'sp'))
- grad_value: bfloat16 [32768, 512], P(('grp', 'sp'))
The draws below stay inside these ranges and needn't reach their ends.
Inputs may be any that keep to these rules, and one draw needn't show every extreme that they name: `segment_ids`: ids never fall along the tokens; each document (run of one id) has at most 2048 tokens, and one has exactly 2048.
All inputs are finite; a program needn't handle non-finite values.
Results may differ from the reference program's by a relative error of at most 0.012.
Values may be sent and summed in bfloat16 or wider, within the bound.
A program may use at most 128 MiB of HBM per device.

```python
import math
import jax
import jax.numpy as jnp
import numpy as np
from jax import lax

QUERY_HEADS = 48
KEY_VALUE_HEADS = 4
HEAD_SIZE = 128
TOK_DEV = 128
SEQ = 2048
BLK = 512
TOKEN_TOTAL = 32768
DOCS = 64
N_GRP = 16
N_SP = 16


def draw_query(key, part):
    key = jax.random.fold_in(key, 11)
    random_noise = jax.random.normal(key, (TOKEN_TOTAL, QUERY_HEADS, HEAD_SIZE), jnp.float32)
    return jnp.clip(random_noise, -160.0, 160.0).reshape(TOKEN_TOTAL, QUERY_HEADS * HEAD_SIZE).astype(jnp.bfloat16)


def draw_key(key, part):
    key = jax.random.fold_in(key, 23)
    random_noise = jax.random.normal(key, (TOKEN_TOTAL, KEY_VALUE_HEADS, HEAD_SIZE), jnp.float32)
    return jnp.clip(random_noise, -160.0, 160.0).reshape(TOKEN_TOTAL, KEY_VALUE_HEADS * HEAD_SIZE).astype(jnp.bfloat16)


def draw_grad_out(key, part):
    key = jax.random.fold_in(key, 37)
    first = jax.random.fold_in(key, 0)
    third = jax.random.fold_in(key, 2)
    fourth = jax.random.fold_in(key, 3)
    fifth = jax.random.fold_in(key, 4)
    place = jnp.arange(TOKEN_TOTAL, dtype=jnp.float32) / float(TOKEN_TOTAL)
    order = jax.random.permutation(third, QUERY_HEADS).astype(jnp.float32)
    head_scale = jnp.power(10.0, 0.5 * order / float(QUERY_HEADS - 1))
    common = jax.random.normal(fourth, (TOKEN_TOTAL, HEAD_SIZE), jnp.float32)
    common_weight = jax.random.uniform(fifth, (TOKEN_TOTAL,), jnp.float32, 1.5, 3.0)
    random_noise = jax.random.normal(first, (TOKEN_TOTAL, QUERY_HEADS, HEAD_SIZE), jnp.float32)
    power = place
    scales = jnp.power(10.0, power)
    mixed = random_noise + common_weight[:, None, None] * common[:, None, :]
    mixed = 0.1 * mixed * head_scale[None, :, None] * scales[:, None, None]
    return jnp.clip(mixed, -64.0, 64.0).reshape(TOKEN_TOTAL, QUERY_HEADS * HEAD_SIZE).astype(jnp.bfloat16)


def level_of(key, dims, cuts, low, top_value):
    def one(dim, shards_of):
        heights = jax.random.uniform(jax.random.fold_in(jax.random.fold_in(key, 6), dim), (shards_of,), jnp.float32, low / len(cuts), top_value / len(cuts))
        return jnp.repeat(jnp.exp(heights), dims[dim] // shards_of).reshape((-1,) + (1,) * (len(dims) - dim - 1))

    level = one(*cuts[0])
    for cut in cuts[1:]:
        level = level * one(*cut)
    return level


def length_profile(number_of, total, reach, skew):
    loads = [(1 << 20) // math.isqrt(rank ** skew) + 1 for rank in range(2, number_of + 1)]
    rest, holding = total - reach - (number_of - 1), [1] * (number_of - 1)
    while rest > 0:
        movable = [i for i in range(number_of - 1) if holding[i] < reach]
        whole, left = sum([loads[i] for i in movable]), rest
        for i in movable:
            more = min(reach - holding[i], max(1, left * loads[i] // whole), rest)
            holding[i] = holding[i] + more
            rest = rest - more
    return np.array([reach] + holding)


def uneven(rng, amount, total, limit, lean):
    if amount == 2:
        one = jax.random.randint(rng, (), max(1, total - limit), min(limit, total - 1) + 1)
        return jnp.stack([one, total - one])
    sizes = jnp.asarray(length_profile(amount, total, limit, lean), jnp.int32)
    couples = (amount - 1) // 2
    source_of, taker = sizes[1:1 + 2 * couples:2], sizes[2:2 + 2 * couples:2]
    margin = jnp.minimum(source_of - 1, limit - taker)
    passed = jax.random.randint(jax.random.fold_in(rng, 1), (couples,), 0, 1 << 20) % (margin + 1)
    sizes = sizes.at[1:1 + 2 * couples:2].set(source_of - passed).at[2:2 + 2 * couples:2].set(taker + passed)
    return sizes[jax.random.permutation(jax.random.fold_in(rng, 2), amount)]


def normal_values(stream_key, extent, scale, limit, cuts=(), held_as=jnp.bfloat16):
    values = jax.random.normal(stream_key, extent, jnp.float32) * scale
    if len(cuts) > 0:
        values = level_of(stream_key, extent, cuts, -0.22, 0.18) * values
    return jnp.clip(values, min=-limit, max=limit).astype(held_as)


def setup_inputs(seed: int = 0) -> dict:
    key_of = jax.random.split(jax.random.key(seed), 6)
    return {
        "query": draw_query(jax.random.fold_in(key_of[5], 71), 0),
        "key": draw_key(jax.random.fold_in(key_of[5], 71), 0),
        "value": normal_values(key_of[2], (TOKEN_TOTAL, KEY_VALUE_HEADS * HEAD_SIZE), 1.0, 6.0, ((0, 256),)),
        "grad_out": draw_grad_out(jax.random.fold_in(key_of[5], 71), 0),
        "segment_ids": jnp.searchsorted(jnp.cumsum(uneven(key_of[4], DOCS, TOKEN_TOTAL, SEQ, 2)), jnp.arange(TOKEN_TOTAL), side="right").astype(jnp.int32),
    }


def block_grads(qb, dob, kw, vw, segq, segk, qpos, kpos, scale):
    f32 = jnp.float32
    score = jnp.einsum('qhd,kd->hqk', qb.astype(f32), kw.astype(f32)) * scale
    allowed = (segq[:, None] == segk[None, :]) & (kpos[None, :] <= qpos[:, None])
    score = jnp.where(allowed[None], score, -1e+30)
    top = lax.optimization_barrier(jnp.max(score, axis=2, keepdims=True))
    expo = jnp.exp(score - top)
    prob = expo / lax.optimization_barrier(jnp.sum(expo, axis=2, keepdims=True))
    prob_low = prob.astype(jnp.bfloat16).astype(f32)
    outs = jnp.einsum('hqk,kd->hqd', prob_low, vw.astype(f32))
    delta = lax.optimization_barrier(jnp.sum(jnp.transpose(dob, (1, 0, 2)).astype(f32) * outs, axis=2))
    value_gradient = jnp.einsum('hqk,qhd->kd', prob_low, dob.astype(f32))
    dprob = jnp.einsum('qhd,kd->hqk', dob.astype(f32), vw.astype(f32))
    dscore = (prob * (dprob - delta[:, :, None])).astype(jnp.bfloat16).astype(f32)
    grad_q = jnp.einsum('hqk,kd->qhd', dscore, kw.astype(f32)) * scale
    key_gradient = jnp.einsum('hqk,qhd->kd', dscore, qb.astype(f32)) * scale
    return (grad_q, key_gradient, value_gradient)

def window_pass(q_seq, d_seq, k_seq, v_seq, seg_seq, pack_len, block):
    sequence_input = q_seq.shape[0]
    scale = HEAD_SIZE ** (-0.5)
    seg_seq = seg_seq.astype(jnp.int32)
    key_gradient = jnp.zeros((sequence_input, HEAD_SIZE), jnp.float32)
    value_gradient = jnp.zeros((sequence_input, HEAD_SIZE), jnp.float32)
    pieces = []
    for package in range(sequence_input // pack_len):
        base = package * pack_len
        for index in range(pack_len // block):
            start = base + index * block
            finish = start + block
            qpos = start + jnp.arange(block, dtype=jnp.int32)
            kpos = base + jnp.arange(finish - base, dtype=jnp.int32)
            piece_q, piece_k, piece_v = block_grads(q_seq[start:finish], d_seq[start:finish], k_seq[base:finish], v_seq[base:finish], seg_seq[start:finish], seg_seq[base:finish], qpos, kpos, scale)
            pieces.append(piece_q)
            key_gradient = key_gradient.at[base:finish].add(piece_k)
            value_gradient = value_gradient.at[base:finish].add(piece_v)
    grad_q = jnp.concatenate(pieces, axis=0)
    return (grad_q, key_gradient, value_gradient)

def reference(query, key, value, grad_out, segment_ids):
    model_width = N_SP
    heads_here = QUERY_HEADS // model_width
    repeat_factor = model_width // KEY_VALUE_HEADS
    sequence_input = TOK_DEV * model_width
    q_all = query.reshape(N_GRP, sequence_input, model_width, heads_here, HEAD_SIZE)
    d_all = grad_out.reshape(N_GRP, sequence_input, model_width, heads_here, HEAD_SIZE)
    all_keys = key.reshape(N_GRP, sequence_input, KEY_VALUE_HEADS, HEAD_SIZE)
    all_values = value.reshape(N_GRP, sequence_input, KEY_VALUE_HEADS, HEAD_SIZE)
    s_all = segment_ids.reshape(N_GRP, sequence_input)

    def one_group(items):
        q_g, d_g, k_g, v_g, s_g = items
        q_slots = jnp.transpose(q_g, (1, 0, 2, 3))
        d_slots = jnp.transpose(d_g, (1, 0, 2, 3))
        k_slots = jnp.repeat(jnp.transpose(k_g, (1, 0, 2)), repeat_factor, axis=0)
        v_slots = jnp.repeat(jnp.transpose(v_g, (1, 0, 2)), repeat_factor, axis=0)

        def one_slot(slot):
            return window_pass(slot[0], slot[1], slot[2], slot[3], s_g, SEQ, BLK)
        grad_q, key_gradient, value_gradient = lax.map(one_slot, (q_slots, d_slots, k_slots, v_slots))
        grad_q = grad_q.astype(jnp.bfloat16)
        key_gradient = key_gradient.astype(jnp.bfloat16).astype(jnp.float32).reshape(KEY_VALUE_HEADS, repeat_factor, sequence_input, HEAD_SIZE).sum(axis=1)
        value_gradient = value_gradient.astype(jnp.bfloat16).astype(jnp.float32).reshape(KEY_VALUE_HEADS, repeat_factor, sequence_input, HEAD_SIZE).sum(axis=1)
        grad_q = jnp.transpose(grad_q, (1, 0, 2, 3)).reshape(sequence_input, QUERY_HEADS * HEAD_SIZE)
        key_gradient = jnp.transpose(key_gradient, (1, 0, 2)).reshape(sequence_input, KEY_VALUE_HEADS * HEAD_SIZE)
        value_gradient = jnp.transpose(value_gradient, (1, 0, 2)).reshape(sequence_input, KEY_VALUE_HEADS * HEAD_SIZE)
        return (grad_q, key_gradient, value_gradient)
    grad_q, key_gradient, value_gradient = lax.map(one_group, (q_all, d_all, all_keys, all_values, s_all))
    grad_q = grad_q.reshape(TOKEN_TOTAL, QUERY_HEADS * HEAD_SIZE).astype(jnp.float32)
    key_gradient = key_gradient.reshape(TOKEN_TOTAL, KEY_VALUE_HEADS * HEAD_SIZE)
    value_gradient = value_gradient.reshape(TOKEN_TOTAL, KEY_VALUE_HEADS * HEAD_SIZE)
    total = jnp.sum(grad_q * grad_q) + jnp.sum(key_gradient * key_gradient) + jnp.sum(value_gradient * value_gradient)
    item_count = float(TOKEN_TOTAL * (QUERY_HEADS + 2 * KEY_VALUE_HEADS) * HEAD_SIZE)
    rms = jnp.sqrt(total / item_count + 1e-06)
    return ((grad_q / rms).astype(jnp.bfloat16), (key_gradient / rms).astype(jnp.bfloat16), (value_gradient / rms).astype(jnp.bfloat16))
```

```python
import functools

import jax
import jax.numpy as jnp
from jax import lax
from jax.experimental import pallas as pl
from jax.experimental.pallas import tpu as pltpu
from jax.sharding import PartitionSpec as P

QUERY_HEADS = 48
KEY_VALUE_HEADS = 4
HEAD_SIZE = 128
TOK = 128
N_SP = 16
N_GRP = 16
ROWS = 2 * TOK
SEQ = TOK * N_SP
HALF_Q = QUERY_HEADS * HEAD_SIZE // 2
HALF_KV = KEY_VALUE_HEADS * HEAD_SIZE // 2
CORE_HEADS = QUERY_HEADS // 2
GROUP_HEADS = QUERY_HEADS // KEY_VALUE_HEADS
SCALE = HEAD_SIZE**-0.5
EXP2_SCALE = SCALE * 1.4426950408889634
NEG = -1e30
HB = 4
KB = 256
WIDE = HB * ROWS
ITEMS = float(TOK * N_SP * N_GRP * (QUERY_HEADS + 2 * KEY_VALUE_HEADS) * HEAD_SIZE)

f32 = jnp.float32
bf16 = jnp.bfloat16
MESH = pl.DeviceIdType.MESH


def greet(axis, me, count):
    barrier = pltpu.get_barrier_semaphore()

    def one(d, z):
        other = lax.rem(me + d, count)
        pl.semaphore_signal(barrier, inc=1, device_id={axis: other}, device_id_type=MESH)
        return z

    lax.fori_loop(1, count, one, 0)


def span(index, size):
    return pl.ds(pl.multiple_of(index * size, size), size)


def gather_kernel(q, do, k, v, seg, q2, do2, k2, v2, seg2, far_send, far_recv, near_send, near_recv, here):
    me = lax.axis_index("sp")
    core = lax.rem(me, 2)
    row = me // 4
    peer = me + 1 - 2 * core
    greet("sp", me, N_SP)
    mine, theirs = span(core, HALF_Q), span(1 - core, HALF_Q)
    rows = span(me, TOK)
    kv_mine = span(core, HALF_KV)
    local = [
        pltpu.make_async_copy(q.at[:, mine], q2.at[span(core, TOK), :], here.at[0]),
        pltpu.make_async_copy(do.at[:, mine], do2.at[span(core, TOK), :], here.at[1]),
        pltpu.make_async_copy(k.at[:, kv_mine], k2.at[rows, :], here.at[2]),
        pltpu.make_async_copy(v.at[:, kv_mine], v2.at[rows, :], here.at[3]),
        pltpu.make_async_copy(seg, seg2.at[me], here.at[4]),
    ]
    for copy in local:
        copy.start()
    pl.semaphore_wait(pltpu.get_barrier_semaphore(), N_SP - 1)

    def far(src, target):
        lanes = span(lax.rem(target, 2), HALF_KV)
        part = span(src, TOK)
        pairs = (
            (k.at[:, lanes], k2.at[part, :]),
            (v.at[:, lanes], v2.at[part, :]),
            (seg, seg2.at[src]),
        )
        return [
            pltpu.make_async_remote_copy(
                src_ref=a,
                dst_ref=b,
                send_sem=far_send.at[n, target],
                recv_sem=far_recv.at[n, src],
                device_id={"sp": target},
                device_id_type=MESH,
            )
            for n, (a, b) in enumerate(pairs)
        ]

    near = [
        pltpu.make_async_remote_copy(
            src_ref=a.at[:, theirs],
            dst_ref=b.at[span(core, TOK), :],
            send_sem=near_send.at[n],
            recv_sem=near_recv.at[n],
            device_id={"sp": peer},
            device_id_type=MESH,
        )
        for n, (a, b) in enumerate(((q, q2), (do, do2)))
    ]

    def send(d, z):
        target = lax.rem(me + d, N_SP)

        @pl.when(target // 4 >= row)
        def _():
            for copy in far(me, target):
                copy.start()

        return z

    lax.fori_loop(1, N_SP, send, 0)
    for copy in near:
        copy.start()
    for copy in local:
        copy.wait()
    for copy in near:
        copy.wait()

    def finish(d, z):
        other = lax.rem(me + d, N_SP)

        @pl.when(other // 4 >= row)
        def _():
            for copy in far(me, other):
                copy.wait_send()

        @pl.when(other // 4 <= row)
        def _():
            for copy in far(other, me):
                copy.wait_recv()

        return z

    lax.fori_loop(1, N_SP, finish, 0)


def gather(query, grad_out, key, value, seg):
    any_spec = pl.BlockSpec(memory_space=pl.ANY)
    return pl.pallas_call(
        gather_kernel,
        out_shape=(
            jax.ShapeDtypeStruct((ROWS, HALF_Q), bf16),
            jax.ShapeDtypeStruct((ROWS, HALF_Q), bf16),
            jax.ShapeDtypeStruct((SEQ, HALF_KV), bf16),
            jax.ShapeDtypeStruct((SEQ, HALF_KV), bf16),
            jax.ShapeDtypeStruct((N_SP, 1, TOK), jnp.int32),
        ),
        in_specs=[any_spec] * 5,
        out_specs=[any_spec] * 5,
        scratch_shapes=[
            pltpu.SemaphoreType.DMA((3, N_SP)),
            pltpu.SemaphoreType.DMA((3, N_SP)),
            pltpu.SemaphoreType.DMA((2,)),
            pltpu.SemaphoreType.DMA((2,)),
            pltpu.SemaphoreType.DMA((5,)),
        ],
        compiler_params=pltpu.CompilerParams(collective_id=0, has_side_effects=True),
        name="gather_kv_swap_q",
    )(query, grad_out, key, value, seg)


def nt(a, b):
    return lax.dot_general(a, b, (((1,), (1,)), ((), ())), preferred_element_type=f32)


def nn(a, b):
    return lax.dot_general(a, b, (((1,), (0,)), ((), ())), preferred_element_type=f32)


def attend(blocks, chip, q, do, k, v, seg, dq, dk, dv, s_s, e_s, dp_s, dk_s, dv_s, kt, kaug, qoh):
    keys = blocks * KB
    lane = lax.broadcasted_iota(jnp.int32, (TOK, TOK), 1).astype(f32)

    def ids(index):
        line = jnp.broadcast_to(seg[index].astype(f32), (TOK, TOK))
        return line.T

    dk_s[0:keys, :] = jnp.zeros((keys, HALF_KV), f32)
    dv_s[0:keys, :] = jnp.zeros((keys, HALF_KV), f32)
    for h in range(2):
        lanes = slice(h * HEAD_SIZE, (h + 1) * HEAD_SIZE)
        kt[h, :, 0:keys] = k[0:keys, lanes].T
        kaug[h, 0:keys, 0:HEAD_SIZE] = k[0:keys, lanes]
    for n in range(keys // TOK):
        bias = jnp.where(ids(n) == lane, 0.0, NEG).astype(bf16)
        for h in range(2):
            kaug[h, n * TOK : (n + 1) * TOK, HEAD_SIZE:] = bias
    for c in range(2):
        qoh[c * TOK : (c + 1) * TOK, :] = jnp.where(ids(2 * chip + c) == lane, 1.0, 0.0).astype(bf16)
    place = lax.broadcasted_iota(jnp.int32, (KB, WIDE), 0)
    token = lax.broadcasted_iota(jnp.int32, (1, ROWS), 1) + chip * ROWS
    token = jnp.concatenate([token] * HB, axis=1)

    def heads(t, z):
        head = t * HB // GROUP_HEADS
        lanes = span(head, HEAD_SIZE)
        cols = [span(t * HB + j, HEAD_SIZE) for j in range(HB)]
        qt = jnp.concatenate([q[:, c] for c in cols], axis=0)
        dt = jnp.concatenate([do[:, c] for c in cols], axis=0)
        qa = jnp.concatenate([qt, jnp.concatenate([qoh[...]] * HB, axis=0)], axis=1)
        top = None
        for b in range(blocks):
            part = slice(b * KB, (b + 1) * KB)
            s = nt(kaug[head, part, :], qa)
            if b >= blocks - 2:
                s = jnp.where(place + b * KB <= token, s, NEG)
            s_s[part, :] = s
            high = jnp.max(s, axis=0, keepdims=True)
            top = high if top is None else jnp.maximum(top, high)
        total = jnp.zeros((1, WIDE), f32)
        delta = jnp.zeros((1, WIDE), f32)
        for b in range(blocks):
            part = slice(b * KB, (b + 1) * KB)
            dp = nt(v[part, lanes], dt)
            e = jnp.exp2((s_s[part, :] - top) * EXP2_SCALE)
            total = total + jnp.sum(e, axis=0, keepdims=True)
            delta = delta + jnp.sum(e * dp, axis=0, keepdims=True)
            e_s[part, :] = e.astype(bf16)
            dp_s[part, :] = dp.astype(bf16)
        inverse = 1.0 / total
        delta = (delta * inverse).astype(bf16)
        inverse = inverse.astype(bf16)
        acc = None
        for b in range(blocks):
            part = slice(b * KB, (b + 1) * KB)
            p = e_s[part, :] * inverse
            ds = p * (dp_s[part, :] - delta)
            dv_s[part, lanes] += nn(p, dt)
            dk_s[part, lanes] += nn(ds, qt)
            x = nn(kt[head, :, part], ds)
            acc = x if acc is None else acc + x
        out = (acc * SCALE).T.astype(bf16)
        for j in range(HB):
            dq[:, cols[j]] = out[j * ROWS : (j + 1) * ROWS]
        return z

    lax.fori_loop(0, CORE_HEADS // HB, heads, 0)
    dk[0:keys, :] = (dk_s[0:keys, :] * SCALE).astype(bf16)
    dv[0:keys, :] = dv_s[0:keys, :].astype(bf16)


def attention_kernel(*refs):
    me = lax.axis_index("sp")
    chip = me // 2
    for row in range(N_SP // 4):
        pl.when(me // 4 == row)(functools.partial(attend, 2 * (row + 1), chip, *refs))


def attention(q2, do2, k2, v2, seg2):
    vmem = pltpu.VMEM
    spec = pl.BlockSpec(memory_space=vmem)
    return pl.pallas_call(
        attention_kernel,
        out_shape=(
            jax.ShapeDtypeStruct((ROWS, HALF_Q), bf16),
            jax.ShapeDtypeStruct((SEQ, HALF_KV), bf16),
            jax.ShapeDtypeStruct((SEQ, HALF_KV), bf16),
        ),
        in_specs=[spec] * 5,
        out_specs=[spec] * 3,
        scratch_shapes=[
            vmem((SEQ, WIDE), f32),
            vmem((SEQ, WIDE), bf16),
            vmem((SEQ, WIDE), bf16),
            vmem((SEQ, HALF_KV), f32),
            vmem((SEQ, HALF_KV), f32),
            vmem((2, HEAD_SIZE, SEQ), bf16),
            vmem((2, SEQ, 2 * HEAD_SIZE), bf16),
            vmem((ROWS, HEAD_SIZE), bf16),
        ],
        compiler_params=pltpu.CompilerParams(vmem_limit_bytes=58 << 20),
        name="attention_grads",
    )(q2, do2, k2, v2, seg2)


def finish_kernel(
    dq, dk, dv, gq, gk, gv, dq_in, dk_in, dv_in, k_sum, v_sum, sq_mine, sq_sp, sq_grp,
    near_send, near_recv, far_send, far_recv, here, sp_send, sp_recv, grp_send, grp_recv,
):
    me = lax.axis_index("sp")
    group = lax.axis_index("grp")
    core = lax.rem(me, 2)
    chip = me // 2
    peer = me + 1 - 2 * core
    greet("sp", me, N_SP)
    greet("grp", group, N_GRP)
    pl.semaphore_wait(pltpu.get_barrier_semaphore(), N_SP + N_GRP - 2)

    def far(src, target):
        part = span(target, TOK)
        return [
            pltpu.make_async_remote_copy(
                src_ref=a.at[part, :],
                dst_ref=b.at[src],
                send_sem=far_send.at[n, target],
                recv_sem=far_recv.at[n, src],
                device_id={"sp": target},
                device_id_type=MESH,
            )
            for n, (a, b) in enumerate(((dk, dk_in), (dv, dv_in)))
        ]

    near = pltpu.make_async_remote_copy(
        src_ref=dq.at[span(1 - core, TOK), :],
        dst_ref=dq_in,
        send_sem=near_send,
        recv_sem=near_recv,
        device_id={"sp": peer},
        device_id_type=MESH,
    )
    local = [
        pltpu.make_async_copy(dk.at[span(me, TOK), :], dk_in.at[me], here.at[0]),
        pltpu.make_async_copy(dv.at[span(me, TOK), :], dv_in.at[me], here.at[1]),
    ]

    def send(d, z):
        target = lax.rem(me + d, N_SP)

        @pl.when(target // 2 <= chip)
        def _():
            for copy in far(me, target):
                copy.start()

        return z

    lax.fori_loop(1, N_SP, send, 0)
    near.start()
    for copy in local:
        copy.start()
    for copy in local:
        copy.wait()

    def square(x):
        x = x.astype(f32)
        return jnp.sum(x * x)

    own = dq.at[span(core, TOK), :]
    squares = square(own[...])
    near.wait()
    squares += square(dq_in[...])

    def arrive(d, z):
        other = lax.rem(me + d, N_SP)

        @pl.when(other // 2 >= chip)
        def _():
            for copy in far(other, me):
                copy.wait_recv()

        @pl.when(other // 2 <= chip)
        def _():
            for copy in far(me, other):
                copy.wait_send()

        return z

    lax.fori_loop(1, N_SP, arrive, 0)
    k_sum[...] = jnp.zeros_like(k_sum)
    v_sum[...] = jnp.zeros_like(v_sum)

    def add(j, z):
        for c in range(2):
            lanes = slice(c * HALF_KV, (c + 1) * HALF_KV)
            k_sum[:, lanes] += dk_in[2 * j + c].astype(f32)
            v_sum[:, lanes] += dv_in[2 * j + c].astype(f32)
        return z

    lax.fori_loop(chip, N_SP // 2, add, 0)
    squares += square(k_sum[...]) + square(v_sum[...])
    for axis, index, count, slots, sends, recvs in (
        ("sp", me, N_SP, sq_sp, sp_send, sp_recv),
        ("grp", group, N_GRP, sq_grp, grp_send, grp_recv),
    ):
        stage = 0 if axis == "sp" else 1
        sq_mine[stage] = jnp.full((8, 128), squares, f32)

        def message(src, target):
            return pltpu.make_async_remote_copy(
                src_ref=sq_mine.at[stage],
                dst_ref=slots.at[src],
                send_sem=sends.at[target],
                recv_sem=recvs.at[src],
                device_id={axis: target},
                device_id_type=MESH,
            )

        def start(d, z):
            message(index, lax.rem(index + d, count)).start()
            return z

        def wait(d, z):
            other = lax.rem(index + d, count)
            message(index, other).wait_send()
            message(other, index).wait_recv()
            return z

        lax.fori_loop(1, count, start, 0)
        slots[index] = sq_mine[stage]
        lax.fori_loop(1, count, wait, 0)
        tile = jnp.sum(slots[...], axis=0)
        squares = jnp.max(tile)
    factor = 1.0 / jnp.sqrt(jnp.full((8, 128), squares, f32) / ITEMS + 1e-6)
    factor = factor[0:1, 0:1]
    gq[:, span(core, HALF_Q)] = (own[...].astype(f32) * factor).astype(bf16)
    gq[:, span(1 - core, HALF_Q)] = (dq_in[...].astype(f32) * factor).astype(bf16)
    gk[...] = (k_sum[...] * factor).astype(bf16)
    gv[...] = (v_sum[...] * factor).astype(bf16)


def finish(dq, dk, dv):
    vmem = pltpu.VMEM
    spec = pl.BlockSpec(memory_space=vmem)
    sems = pltpu.SemaphoreType.DMA
    width = KEY_VALUE_HEADS * HEAD_SIZE
    return pl.pallas_call(
        finish_kernel,
        out_shape=(
            jax.ShapeDtypeStruct((TOK, QUERY_HEADS * HEAD_SIZE), bf16),
            jax.ShapeDtypeStruct((TOK, width), bf16),
            jax.ShapeDtypeStruct((TOK, width), bf16),
        ),
        in_specs=[spec] * 3,
        out_specs=[spec] * 3,
        scratch_shapes=[
            vmem((TOK, HALF_Q), bf16),
            vmem((N_SP, TOK, HALF_KV), bf16),
            vmem((N_SP, TOK, HALF_KV), bf16),
            vmem((TOK, width), f32),
            vmem((TOK, width), f32),
            vmem((2, 8, 128), f32),
            vmem((N_SP, 8, 128), f32),
            vmem((N_GRP, 8, 128), f32),
            sems(()),
            sems(()),
            sems((2, N_SP)),
            sems((2, N_SP)),
            sems((2,)),
            sems((N_SP,)),
            sems((N_SP,)),
            sems((N_GRP,)),
            sems((N_GRP,)),
        ],
        compiler_params=pltpu.CompilerParams(
            collective_id=1, has_side_effects=True, vmem_limit_bytes=40 << 20
        ),
        name="reduce_and_scale",
    )(dq, dk, dv)


def on_device(query, key, value, grad_out, segment_ids):
    moved = gather(query, grad_out, key, value, segment_ids.reshape(1, TOK))
    return finish(*attention(*moved))


def solution(mesh):
    whole = P(("grp", "sp"), None)
    return jax.shard_map(
        on_device,
        mesh=mesh,
        in_specs=(whole, whole, whole, whole, P(("grp", "sp"))),
        out_specs=(whole, whole, whole),
        check_vma=False,
    )
```

```python
import functools

import jax
import jax.numpy as jnp
from jax import lax
from jax.experimental import pallas as pl
from jax.experimental.pallas import tpu as pltpu
from jax.sharding import PartitionSpec as P

QUERY_HEADS = 48
KEY_VALUE_HEADS = 4
HEAD_SIZE = 128
TOK = 128
N_SP = 16
N_GRP = 16
ROWS = 2 * TOK
SEQ = TOK * N_SP
HALF_Q = QUERY_HEADS * HEAD_SIZE // 2
HALF_KV = KEY_VALUE_HEADS * HEAD_SIZE // 2
CORE_HEADS = QUERY_HEADS // 2
GROUP_HEADS = QUERY_HEADS // KEY_VALUE_HEADS
SCALE = HEAD_SIZE**-0.5
EXP2_SCALE = SCALE * 1.4426950408889634
NEG = -1e30
HB = 4
GROUPS = GROUP_HEADS // HB
KB = 256
WIDE = HB * ROWS
ITEMS = float(TOK * N_SP * N_GRP * (QUERY_HEADS + 2 * KEY_VALUE_HEADS) * HEAD_SIZE)

f32 = jnp.float32
bf16 = jnp.bfloat16
MESH = pl.DeviceIdType.MESH


def greet(axis, me, count):
    barrier = pltpu.get_barrier_semaphore()

    def one(d, z):
        other = lax.rem(me + d, count)
        pl.semaphore_signal(barrier, inc=1, device_id={axis: other}, device_id_type=MESH)
        return z

    lax.fori_loop(1, count, one, 0)


def span(index, size):
    return pl.ds(pl.multiple_of(index * size, size), size)


def nt(a, b):
    return lax.dot_general(a, b, (((1,), (1,)), ((), ())), preferred_element_type=f32)


def nn(a, b):
    return lax.dot_general(a, b, (((1,), (0,)), ((), ())), preferred_element_type=f32)


def attend(blocks, chip, h, q, do, v, seg, dq, s_s, e_s, dp_s, dk_s, dv_s, kt, kaug, qoh, dk_out, dv_out, done):
    keys = blocks * KB
    lane = lax.broadcasted_iota(jnp.int32, (TOK, TOK), 1).astype(f32)

    def ids(index):
        line = jnp.broadcast_to(seg[index].astype(f32), (TOK, TOK))
        return line.T

    dk_s[0:keys, :] = jnp.zeros((keys, HEAD_SIZE), f32)
    dv_s[0:keys, :] = jnp.zeros((keys, HEAD_SIZE), f32)

    def prepare(n, z):
        part = span(n, TOK)
        kt[:, part] = kaug[h, part, 0:HEAD_SIZE].T
        kaug[h, part, HEAD_SIZE:] = jnp.where(ids(n) == lane, 0.0, NEG).astype(bf16)
        return z

    lax.fori_loop(0, keys // TOK, prepare, 0)
    for c in range(2):
        qoh[c * TOK : (c + 1) * TOK, :] = jnp.where(ids(2 * chip + c) == lane, 1.0, 0.0).astype(bf16)
    place = lax.broadcasted_iota(jnp.int32, (KB, WIDE), 0)
    token = lax.broadcasted_iota(jnp.int32, (1, ROWS), 1) + chip * ROWS
    token = jnp.concatenate([token] * HB, axis=1)

    def heads(t, z):
        group = h * GROUPS + t
        cols = [span(group * HB + j, HEAD_SIZE) for j in range(HB)]
        qt = jnp.concatenate([q[:, c] for c in cols], axis=0)
        dt = jnp.concatenate([do[:, c] for c in cols], axis=0)
        qa = jnp.concatenate([qt, jnp.concatenate([qoh[...]] * HB, axis=0)], axis=1)
        top = None
        for b in range(blocks):
            part = slice(b * KB, (b + 1) * KB)
            s = nt(kaug[h, part, :], qa)
            if b >= blocks - 2:
                s = jnp.where(place + b * KB <= token, s, NEG)
            s_s[part, :] = s
            high = jnp.max(s, axis=0, keepdims=True)
            top = high if top is None else jnp.maximum(top, high)
        total = jnp.zeros((1, WIDE), f32)
        delta = jnp.zeros((1, WIDE), f32)
        for b in range(blocks):
            part = slice(b * KB, (b + 1) * KB)
            dp = nt(v[h, part, :], dt)
            e = jnp.exp2((s_s[part, :] - top) * EXP2_SCALE)
            total = total + jnp.sum(e, axis=0, keepdims=True)
            delta = delta + jnp.sum(e * dp, axis=0, keepdims=True)
            e_s[part, :] = e.astype(bf16)
            dp_s[part, :] = dp.astype(bf16)
        inverse = 1.0 / total
        delta = (delta * inverse).astype(bf16)
        inverse = inverse.astype(bf16)
        acc = None
        for b in range(blocks):
            part = slice(b * KB, (b + 1) * KB)
            p = e_s[part, :] * inverse
            ds = p * (dp_s[part, :] - delta)
            dv_s[part, :] += nn(p, dt)
            dk_s[part, :] += nn(ds, qt)
            x = nn(kt[:, part], ds)
            acc = x if acc is None else acc + x
        out = (acc * SCALE).T.astype(bf16)
        for j in range(HB):
            dq[:, cols[j]] = out[j * ROWS : (j + 1) * ROWS]
        done(group)
        return z

    lax.fori_loop(0, GROUPS, heads, 0)
    dk_out[h, 0:keys, :] = (dk_s[0:keys, :] * SCALE).astype(bf16)
    dv_out[h, 0:keys, :] = dv_s[0:keys, :].astype(bf16)


def kernel(
    q, do, k, v, seg, gq, gk, gv,
    q2, do2, v2, seg2, dq2, s_s, e_s, dp_s, dk_s, dv_s, kt, kaug, qoh, dk_out, dv_out,
    dq_in, dk_in, dv_in, k_sum, v_sum, sq_mine, sq_sp, sq_grp,
    here, near_send, near_recv, far_send, far_recv, back_send, back_recv, dq_send, dq_recv,
    sp_send, sp_recv, grp_send, grp_recv,
):
    me = lax.axis_index("sp")
    group = lax.axis_index("grp")
    core = lax.rem(me, 2)
    chip = me // 2
    row = me // 4
    peer = me + 1 - 2 * core

    def remote(src, dst, send, recv, target):
        return pltpu.make_async_remote_copy(
            src_ref=src, dst_ref=dst, send_sem=send, recv_sem=recv, device_id={"sp": target}, device_id_type=MESH
        )

    def near(h):
        lanes = span((1 - core) * 2 + h, HALF_Q // 2)
        to = span(h, HALF_Q // 2)
        return [
            remote(a.at[:, lanes], b.at[span(core, TOK), to], near_send.at[n, h], near_recv.at[n, h], peer)
            for n, (a, b) in enumerate(((q, q2), (do, do2)))
        ]

    def far(h, src, target):
        lanes = span(lax.rem(target, 2) * 2 + h, HEAD_SIZE)
        part = span(src, TOK)
        return [
            remote(a.at[:, lanes], b, far_send.at[n, h, target], far_recv.at[n, h, src], target)
            for n, (a, b) in enumerate(((k, kaug.at[h, part, 0:HEAD_SIZE]), (v, v2.at[h, part, :])))
        ]

    def ids(src, target):
        return remote(seg, seg2.at[src], far_send.at[2, 0, target], far_recv.at[2, 0, src], target)

    def back(h, src, target):
        part = span(target, TOK)
        return [
            remote(a.at[h, part, :], b.at[src, h], back_send.at[n, h, target], back_recv.at[n, h, src], target)
            for n, (a, b) in enumerate(((dk_out, dk_in), (dv_out, dv_in)))
        ]

    def back_near(g):
        lanes = span(g, HB * HEAD_SIZE)
        return remote(dq2.at[span(1 - core, TOK), lanes], dq_in.at[:, lanes], dq_send.at[g], dq_recv.at[g], peer)

    greet("sp", me, N_SP)
    greet("grp", group, N_GRP)
    local = []
    for h in range(2):
        half = span(core * 2 + h, HALF_Q // 2)
        to = span(h, HALF_Q // 2)
        lanes = span(core * 2 + h, HEAD_SIZE)
        local.append(
            [
                pltpu.make_async_copy(q.at[:, half], q2.at[span(core, TOK), to], here.at[0, h]),
                pltpu.make_async_copy(do.at[:, half], do2.at[span(core, TOK), to], here.at[1, h]),
                pltpu.make_async_copy(k.at[:, lanes], kaug.at[h, span(me, TOK), 0:HEAD_SIZE], here.at[2, h]),
                pltpu.make_async_copy(v.at[:, lanes], v2.at[h, span(me, TOK), :], here.at[3, h]),
            ]
        )
    local[0].append(pltpu.make_async_copy(seg, seg2.at[me], here.at[4, 0]))
    pl.semaphore_wait(pltpu.get_barrier_semaphore(), N_SP + N_GRP - 2)
    for h in range(2):
        for copy in near(h):
            copy.start()
        for copy in local[h]:
            copy.start()

        def send(d, z):
            target = lax.rem(me + d, N_SP)

            @pl.when(target // 4 >= row)
            def _():
                for copy in far(h, me, target):
                    copy.start()
                if h == 0:
                    ids(me, target).start()

            return z

        lax.fori_loop(1, N_SP, send, 0)

    for h in range(2):
        for copy in local[h]:
            copy.wait()
        for copy in near(h):
            copy.wait_recv()

        def arrive(d, z):
            other = lax.rem(me + d, N_SP)

            @pl.when(other // 4 <= row)
            def _():
                for copy in far(h, other, me):
                    copy.wait_recv()
                if h == 0:
                    ids(other, me).wait_recv()

            return z

        lax.fori_loop(1, N_SP, arrive, 0)
        for n in range(N_SP // 4):
            work = functools.partial(
                attend, 2 * (n + 1), chip, h, q2, do2, v2, seg2, dq2, s_s, e_s, dp_s, dk_s, dv_s, kt, kaug, qoh,
                dk_out, dv_out, lambda g: back_near(g).start(),
            )
            pl.when(row == n)(work)

        def give(d, z):
            target = lax.rem(me + d, N_SP)

            @pl.when(target // 2 <= chip)
            def _():
                for copy in back(h, me, target):
                    copy.start()

            return z

        lax.fori_loop(1, N_SP, give, 0)

    def square(x):
        x = x.astype(f32)
        return jnp.sum(x * x)

    def settle(d, z):
        other = lax.rem(me + d, N_SP)

        @pl.when(other // 4 >= row)
        def _():
            for h in range(2):
                for copy in far(h, me, other):
                    copy.wait_send()
            ids(me, other).wait_send()

        return z

    lax.fori_loop(1, N_SP, settle, 0)
    for h in range(2):
        for copy in near(h):
            copy.wait_send()
    own = dq2.at[span(core, TOK), :]
    squares = square(own[...])

    def halves(g, z):
        back_near(g).wait()
        return z

    lax.fori_loop(0, 2 * GROUPS, halves, 0)
    squares += square(dq_in[...])
    for c in range(2):
        for h in range(2):
            lanes = slice((2 * c + h) * HEAD_SIZE, (2 * c + h + 1) * HEAD_SIZE)
            k_sum[:, lanes] = jnp.zeros((TOK, HEAD_SIZE), f32)
            v_sum[:, lanes] = jnp.zeros((TOK, HEAD_SIZE), f32)

            @pl.when(core == c)
            def _():
                k_sum[:, lanes] = dk_out[h, span(me, TOK), :].astype(f32)
                v_sum[:, lanes] = dv_out[h, span(me, TOK), :].astype(f32)

    for h in range(2):

        def add(j, z):
            for c in range(2):
                other = 2 * j + c

                @pl.when(other != me)
                def _():
                    for copy in back(h, other, me):
                        copy.wait_recv()
                    lanes = slice((2 * c + h) * HEAD_SIZE, (2 * c + h + 1) * HEAD_SIZE)
                    k_sum[:, lanes] += dk_in[other, h].astype(f32)
                    v_sum[:, lanes] += dv_in[other, h].astype(f32)

            return z

        lax.fori_loop(chip, N_SP // 2, add, 0)
    squares += square(k_sum[...]) + square(v_sum[...])
    for axis, index, count, slots, sends, recvs in (
        ("sp", me, N_SP, sq_sp, sp_send, sp_recv),
        ("grp", group, N_GRP, sq_grp, grp_send, grp_recv),
    ):
        stage = 0 if axis == "sp" else 1
        sq_mine[stage] = jnp.full((8, 128), squares, f32)

        def message(src, target):
            return pltpu.make_async_remote_copy(
                src_ref=sq_mine.at[stage],
                dst_ref=slots.at[src],
                send_sem=sends.at[target],
                recv_sem=recvs.at[src],
                device_id={axis: target},
                device_id_type=MESH,
            )

        def start(d, z):
            message(index, lax.rem(index + d, count)).start()
            return z

        def wait(d, z):
            other = lax.rem(index + d, count)
            message(index, other).wait_send()
            message(other, index).wait_recv()
            return z

        lax.fori_loop(1, count, start, 0)
        slots[index] = sq_mine[stage]
        lax.fori_loop(1, count, wait, 0)
        tile = jnp.sum(slots[...], axis=0)
        squares = jnp.max(tile)

    def given(d, z):
        target = lax.rem(me + d, N_SP)

        @pl.when(target // 2 <= chip)
        def _():
            for h in range(2):
                for copy in back(h, me, target):
                    copy.wait_send()

        return z

    lax.fori_loop(1, N_SP, given, 0)
    factor = 1.0 / jnp.sqrt(jnp.full((8, 128), squares, f32) / ITEMS + 1e-6)
    factor = factor[0:1, 0:1]
    gq[:, span(core, HALF_Q)] = (own[...].astype(f32) * factor).astype(bf16)
    gq[:, span(1 - core, HALF_Q)] = (dq_in[...].astype(f32) * factor).astype(bf16)
    gk[...] = (k_sum[...] * factor).astype(bf16)
    gv[...] = (v_sum[...] * factor).astype(bf16)


def on_device(query, key, value, grad_out, segment_ids):
    vmem = pltpu.VMEM
    sems = pltpu.SemaphoreType.DMA
    width = KEY_VALUE_HEADS * HEAD_SIZE
    return pl.pallas_call(
        kernel,
        out_shape=(
            jax.ShapeDtypeStruct((TOK, QUERY_HEADS * HEAD_SIZE), bf16),
            jax.ShapeDtypeStruct((TOK, width), bf16),
            jax.ShapeDtypeStruct((TOK, width), bf16),
        ),
        in_specs=[pl.BlockSpec(memory_space=pl.ANY)] * 5,
        out_specs=[pl.BlockSpec(memory_space=vmem)] * 3,
        scratch_shapes=[
            vmem((ROWS, HALF_Q), bf16),
            vmem((ROWS, HALF_Q), bf16),
            vmem((2, SEQ, HEAD_SIZE), bf16),
            vmem((N_SP, 1, TOK), jnp.int32),
            vmem((ROWS, HALF_Q), bf16),
            vmem((SEQ, WIDE), f32),
            vmem((SEQ, WIDE), bf16),
            vmem((SEQ, WIDE), bf16),
            vmem((SEQ, HEAD_SIZE), f32),
            vmem((SEQ, HEAD_SIZE), f32),
            vmem((HEAD_SIZE, SEQ), bf16),
            vmem((2, SEQ, 2 * HEAD_SIZE), bf16),
            vmem((ROWS, HEAD_SIZE), bf16),
            vmem((2, SEQ, HEAD_SIZE), bf16),
            vmem((2, SEQ, HEAD_SIZE), bf16),
            vmem((TOK, HALF_Q), bf16),
            vmem((N_SP, 2, TOK, HEAD_SIZE), bf16),
            vmem((N_SP, 2, TOK, HEAD_SIZE), bf16),
            vmem((TOK, width), f32),
            vmem((TOK, width), f32),
            vmem((2, 8, 128), f32),
            vmem((N_SP, 8, 128), f32),
            vmem((N_GRP, 8, 128), f32),
            sems((5, 2)),
            sems((2, 2)),
            sems((2, 2)),
            sems((3, 2, N_SP)),
            sems((3, 2, N_SP)),
            sems((2, 2, N_SP)),
            sems((2, 2, N_SP)),
            sems((2 * GROUPS,)),
            sems((2 * GROUPS,)),
            sems((N_SP,)),
            sems((N_SP,)),
            sems((N_GRP,)),
            sems((N_GRP,)),
        ],
        compiler_params=pltpu.CompilerParams(
            collective_id=0, has_side_effects=True, vmem_limit_bytes=58 << 20
        ),
        name="attention_grads",
    )(query, grad_out, key, value, segment_ids.reshape(1, TOK))


def solution(mesh):
    whole = P(("grp", "sp"), None)
    return jax.shard_map(
        on_device,
        mesh=mesh,
        in_specs=(whole, whole, whole, whole, P(("grp", "sp"))),
        out_specs=(whole, whole, whole),
        check_vma=False,
    )
```

```python
import functools

import jax
import jax.numpy as jnp
from jax import lax
from jax.experimental import pallas as pl
from jax.experimental.pallas import tpu as pltpu
from jax.sharding import PartitionSpec as P

QUERY_HEADS = 48
KEY_VALUE_HEADS = 4
HEAD_SIZE = 128
TOK = 128
N_SP = 16
N_GRP = 16
ROWS = 2 * TOK
SEQ = TOK * N_SP
HALF_Q = QUERY_HEADS * HEAD_SIZE // 2
HALF_KV = KEY_VALUE_HEADS * HEAD_SIZE // 2
CORE_HEADS = QUERY_HEADS // 2
GROUP_HEADS = QUERY_HEADS // KEY_VALUE_HEADS
SCALE = HEAD_SIZE**-0.5
EXP2_SCALE = SCALE * 1.4426950408889634
NEG = -1e30
HB = 4
GROUPS = GROUP_HEADS // HB
KB = 256
ROW_KEYS = 4 * TOK
WIDE = HB * ROWS
ALL = GROUP_HEADS * ROWS
ITEMS = float(TOK * N_SP * N_GRP * (QUERY_HEADS + 2 * KEY_VALUE_HEADS) * HEAD_SIZE)

f32 = jnp.float32
bf16 = jnp.bfloat16
MESH = pl.DeviceIdType.MESH


def greet(axis, me, count):
    barrier = pltpu.get_barrier_semaphore()

    def one(d, z):
        other = lax.rem(me + d, count)
        pl.semaphore_signal(barrier, inc=1, device_id={axis: other}, device_id_type=MESH)
        return z

    lax.fori_loop(1, count, one, 0)


def span(index, size):
    return pl.ds(pl.multiple_of(index * size, size), size)


def nt(a, b):
    return lax.dot_general(a, b, (((1,), (1,)), ((), ())), preferred_element_type=f32)


def nn(a, b):
    return lax.dot_general(a, b, (((1,), (0,)), ((), ())), preferred_element_type=f32)


def columns(h, j):
    return span(h * GROUP_HEADS + j, HEAD_SIZE)


def ids_of(seg, index):
    return jnp.broadcast_to(seg[index].astype(f32), (TOK, TOK)).T


def prepare(h, row, seg, kt, kaug):
    lane = lax.broadcasted_iota(jnp.int32, (TOK, TOK), 1).astype(f32)
    for n in range(4):
        part = span(4 * row + n, TOK)
        kt[:, part] = kaug[h, part, 0:HEAD_SIZE].T
        kaug[h, part, HEAD_SIZE:] = jnp.where(ids_of(seg, 4 * row + n) == lane, 0.0, NEG).astype(bf16)


def scores(h, row, chip, diagonal, q, do, v, kaug, qoh, e_s, dp_s, top_s, stat_s):
    for t in range(GROUPS):
        wide = slice(t * WIDE, (t + 1) * WIDE)
        cols = [columns(h, t * HB + j) for j in range(HB)]
        qt = jnp.concatenate([q[:, c] for c in cols], axis=0)
        dt = jnp.concatenate([do[:, c] for c in cols], axis=0)
        qa = jnp.concatenate([qt, jnp.concatenate([qoh[...]] * HB, axis=0)], axis=1)
        top = None if diagonal else stat_s[0:1, wide]
        total = None if diagonal else stat_s[1:2, wide]
        delta = None if diagonal else stat_s[2:3, wide]
        for n in range(ROW_KEYS // KB):
            block = row * (ROW_KEYS // KB) + n
            part = span(block, KB)
            s = nt(kaug[h, part, :], qa)
            dp = nt(v[h, part, :], dt)
            if diagonal:
                place = lax.broadcasted_iota(jnp.int32, (KB, WIDE), 0) + block * KB
                token = lax.broadcasted_iota(jnp.int32, (1, ROWS), 1) + chip * ROWS
                s = jnp.where(place <= jnp.concatenate([token] * HB, axis=1), s, NEG)
            high = jnp.max(s, axis=0, keepdims=True)
            if top is not None:
                high = jnp.maximum(top, high)
                fade = jnp.exp2((top - high) * EXP2_SCALE)
            e = jnp.exp2((s - high) * EXP2_SCALE)
            e_sum = jnp.sum(e, axis=0, keepdims=True)
            d_sum = jnp.sum(e * dp, axis=0, keepdims=True)
            total = e_sum if total is None else total * fade + e_sum
            delta = d_sum if delta is None else delta * fade + d_sum
            top = high
            e_s[part, wide] = e.astype(bf16)
            dp_s[part, wide] = dp.astype(bf16)
            top_s[pl.ds(block, 1), wide] = high
        stat_s[0:1, wide] = top
        stat_s[1:2, wide] = total
        stat_s[2:3, wide] = delta


def grads(h, row, q, do, kt, e_s, dp_s, top_s, stat_s, dqt_s, dk_out, dv_out):
    qt = jnp.concatenate([q[:, columns(h, j)] for j in range(GROUP_HEADS)], axis=0)
    dt = jnp.concatenate([do[:, columns(h, j)] for j in range(GROUP_HEADS)], axis=0)
    top = stat_s[0:1, :]
    inverse = 1.0 / stat_s[1:2, :]
    delta = (stat_s[2:3, :] * inverse).astype(bf16)
    for n in range(ROW_KEYS // KB):
        block = row * (ROW_KEYS // KB) + n
        part = span(block, KB)
        weight = jnp.exp2((top_s[pl.ds(block, 1), :] - top) * EXP2_SCALE) * inverse
        p = e_s[part, :] * weight.astype(bf16)
        ds = p * (dp_s[part, :] - delta)
        dv_out[h, part, :] = nn(p, dt).astype(bf16)
        dk_out[h, part, :] = (nn(ds, qt) * SCALE).astype(bf16)
        dqt_s[...] += nn(kt[:, part], ds)


def kernel(
    q, do, k, v, seg, dq_out, k_sum, v_sum, factor,
    q2, do2, v2, seg2, dq2, e_s, dp_s, top_s, stat_s, dqt_s, kt, kaug, qoh, dk_out, dv_out,
    dq_in, dk_in, dv_in, sq_mine, sq_sp, sq_grp,
    here, near_send, near_recv, far_send, far_recv, back_send, back_recv, dq_send, dq_recv,
    sp_send, sp_recv, grp_send, grp_recv,
):
    me = lax.axis_index("sp")
    group = lax.axis_index("grp")
    core = lax.rem(me, 2)
    chip = me // 2
    row = me // 4
    peer = me + 1 - 2 * core

    def remote(src, dst, send, recv, target):
        return pltpu.make_async_remote_copy(
            src_ref=src, dst_ref=dst, send_sem=send, recv_sem=recv, device_id={"sp": target}, device_id_type=MESH
        )

    def near(h):
        lanes = span((1 - core) * 2 + h, HALF_Q // 2)
        to = span(h, HALF_Q // 2)
        return [
            remote(a.at[:, lanes], b.at[span(core, TOK), to], near_send.at[n, h], near_recv.at[n, h], peer)
            for n, (a, b) in enumerate(((q, q2), (do, do2)))
        ]

    def far(h, src, target):
        lanes = span(lax.rem(target, 2) * 2 + h, HEAD_SIZE)
        part = span(src, TOK)
        return [
            remote(a.at[:, lanes], b, far_send.at[n, h, target], far_recv.at[n, h, src], target)
            for n, (a, b) in enumerate(((k, kaug.at[h, part, 0:HEAD_SIZE]), (v, v2.at[h, part, :])))
        ]

    def ids(src, target):
        return remote(seg, seg2.at[src], far_send.at[2, 0, target], far_recv.at[2, 0, src], target)

    def back(h, src, target):
        part = span(target, TOK)
        return [
            remote(a.at[h, part, :], b.at[src, h], back_send.at[n, h, target], back_recv.at[n, h, src], target)
            for n, (a, b) in enumerate(((dk_out, dk_in), (dv_out, dv_in)))
        ]

    def back_near(h):
        lanes = span(h, HALF_Q // 2)
        return remote(dq2.at[span(1 - core, TOK), lanes], dq_in.at[:, lanes], dq_send.at[h], dq_recv.at[h], peer)

    greet("sp", me, N_SP)
    greet("grp", group, N_GRP)
    def local(h):
        half = span(core * 2 + h, HALF_Q // 2)
        to = span(h, HALF_Q // 2)
        lanes = span(core * 2 + h, HEAD_SIZE)
        return [
            pltpu.make_async_copy(q.at[:, half], q2.at[span(core, TOK), to], here.at[0, h]),
            pltpu.make_async_copy(do.at[:, half], do2.at[span(core, TOK), to], here.at[1, h]),
            pltpu.make_async_copy(k.at[:, lanes], kaug.at[h, span(me, TOK), 0:HEAD_SIZE], here.at[2, h]),
            pltpu.make_async_copy(v.at[:, lanes], v2.at[h, span(me, TOK), :], here.at[3, h]),
        ]

    own_ids = pltpu.make_async_copy(seg, seg2.at[me], here.at[4, 0])
    own_ids.start()
    pl.semaphore_wait(pltpu.get_barrier_semaphore(), N_SP + N_GRP - 2)

    def send_all(h, z):
        for copy in near(h):
            copy.start()
        for copy in local(h):
            copy.start()

        def send(d, z):
            target = lax.rem(me + d, N_SP)

            @pl.when(target // 4 >= row)
            def _():
                for copy in far(h, me, target):
                    copy.start()

                @pl.when(h == 0)
                def _():
                    ids(me, target).start()

            return z

        return lax.fori_loop(1, N_SP, send, z)

    lax.fori_loop(0, 2, send_all, 0)
    own_ids.wait()
    lane = lax.broadcasted_iota(jnp.int32, (TOK, TOK), 1).astype(f32)

    def head(h, z):
        for copy in local(h):
            copy.wait()
        for copy in near(h):
            copy.wait_recv()

        def arrive(at):
            def one(n, z):
                other = 4 * at + n

                @pl.when(other != me)
                def _():
                    for copy in far(h, other, me):
                        copy.wait_recv()

                    @pl.when(h == 0)
                    def _():
                        ids(other, me).wait_recv()

                return z

            lax.fori_loop(0, 4, one, 0)
            prepare(h, at, seg2, kt, kaug)

        arrive(row)

        @pl.when(h == 0)
        def _():
            for c in range(2):
                hot = jnp.where(ids_of(seg2, 2 * chip + c) == lane, 1.0, 0.0)
                qoh[c * TOK : (c + 1) * TOK, :] = hot.astype(bf16)

        common = (q2, do2, v2, kaug, qoh, e_s, dp_s, top_s, stat_s)
        scores(h, row, chip, True, *common)

        def earlier(d, z):
            arrive(row - d)
            scores(h, row - d, chip, False, *common)
            return z

        lax.fori_loop(1, row + 1, earlier, 0)
        dqt_s[...] = jnp.zeros_like(dqt_s)

        def backward(at, z):
            grads(h, at, q2, do2, kt, e_s, dp_s, top_s, stat_s, dqt_s, dk_out, dv_out)

            def give(n, z):
                target = 4 * at + n

                @pl.when((target // 2 <= chip) & (target != me))
                def _():
                    for copy in back(h, me, target):
                        copy.start()

                return z

            return lax.fori_loop(0, 4, give, z)

        lax.fori_loop(0, row + 1, backward, 0)
        for j in range(GROUP_HEADS):
            out = dqt_s[:, j * ROWS : (j + 1) * ROWS] * SCALE
            dq2[:, columns(h, j)] = out.T.astype(bf16)
        back_near(h).start()
        return z

    lax.fori_loop(0, 2, head, 0)

    def square(x):
        x = x.astype(f32)
        return jnp.sum(x * x)

    def settle(d, z):
        other = lax.rem(me + d, N_SP)

        @pl.when(other // 4 >= row)
        def _():
            for h in range(2):
                for copy in far(h, me, other):
                    copy.wait_send()
            ids(me, other).wait_send()

        return z

    lax.fori_loop(1, N_SP, settle, 0)
    for h in range(2):
        for copy in near(h):
            copy.wait_send()
    own = dq2.at[span(core, TOK), :]
    out = [
        pltpu.make_async_copy(own, dq_out.at[:, span(core, HALF_Q)], here.at[0, 0]),
        pltpu.make_async_copy(dq_in, dq_out.at[:, span(1 - core, HALF_Q)], here.at[1, 0]),
    ]
    out[0].start()
    squares = square(own[...])

    def halves(g, z):
        back_near(g).wait()
        return z

    lax.fori_loop(0, 2, halves, 0)
    out[1].start()
    squares += square(dq_in[...])
    for c in range(2):
        for h in range(2):
            lanes = slice((2 * c + h) * HEAD_SIZE, (2 * c + h + 1) * HEAD_SIZE)
            k_sum[:, lanes] = jnp.zeros((TOK, HEAD_SIZE), f32)
            v_sum[:, lanes] = jnp.zeros((TOK, HEAD_SIZE), f32)

            @pl.when(core == c)
            def _():
                k_sum[:, lanes] = dk_out[h, span(me, TOK), :].astype(f32)
                v_sum[:, lanes] = dv_out[h, span(me, TOK), :].astype(f32)

    for h in range(2):

        def add(j, z):
            for c in range(2):
                other = 2 * j + c

                @pl.when(other != me)
                def _():
                    for copy in back(h, other, me):
                        copy.wait_recv()
                    lanes = slice((2 * c + h) * HEAD_SIZE, (2 * c + h + 1) * HEAD_SIZE)
                    k_sum[:, lanes] += dk_in[other, h].astype(f32)
                    v_sum[:, lanes] += dv_in[other, h].astype(f32)

            return z

        lax.fori_loop(chip, N_SP // 2, add, 0)
    squares += square(k_sum[...]) + square(v_sum[...])
    for axis, index, count, slots, sends, recvs in (
        ("sp", me, N_SP, sq_sp, sp_send, sp_recv),
        ("grp", group, N_GRP, sq_grp, grp_send, grp_recv),
    ):
        stage = 0 if axis == "sp" else 1
        sq_mine[stage] = jnp.full((8, 128), squares, f32)

        def message(src, target):
            return pltpu.make_async_remote_copy(
                src_ref=sq_mine.at[stage],
                dst_ref=slots.at[src],
                send_sem=sends.at[target],
                recv_sem=recvs.at[src],
                device_id={axis: target},
                device_id_type=MESH,
            )

        def start(d, z):
            message(index, lax.rem(index + d, count)).start()
            return z

        def wait(d, z):
            other = lax.rem(index + d, count)
            message(index, other).wait_send()
            message(other, index).wait_recv()
            return z

        lax.fori_loop(1, count, start, 0)
        slots[index] = sq_mine[stage]
        lax.fori_loop(1, count, wait, 0)
        tile = jnp.sum(slots[...], axis=0)
        squares = jnp.max(tile)

    def given(d, z):
        target = lax.rem(me + d, N_SP)

        @pl.when(target // 2 <= chip)
        def _():
            for h in range(2):
                for copy in back(h, me, target):
                    copy.wait_send()

        return z

    lax.fori_loop(1, N_SP, given, 0)
    factor[...] = 1.0 / jnp.sqrt(jnp.full((8, 128), squares, f32) / ITEMS + 1e-6)
    for copy in out:
        copy.wait()


def scale_kernel(dq, dk, dv, factor, gq, gk, gv):
    by = factor[0:1, 0:1]
    gq[...] = (dq[...].astype(f32) * by).astype(bf16)

    @pl.when(pl.program_id(0) == 0)
    def _():
        gk[...] = (dk[...] * by).astype(bf16)
        gv[...] = (dv[...] * by).astype(bf16)


def scale(dq, dk, dv, factor):
    steps = 4
    part = pl.BlockSpec((TOK // steps, dq.shape[1]), lambda i: (i, 0))
    whole = pl.BlockSpec(dk.shape, lambda i: (0, 0))
    return pl.pallas_call(
        scale_kernel,
        grid=(steps,),
        out_shape=tuple(jax.ShapeDtypeStruct(x.shape, bf16) for x in (dq, dk, dv)),
        in_specs=[part, whole, whole, pl.BlockSpec((8, 128), lambda i: (0, 0))],
        out_specs=[part, whole, whole],
        name="scale",
    )(dq, dk, dv, factor)


def on_device(query, key, value, grad_out, segment_ids):
    vmem = pltpu.VMEM
    sems = pltpu.SemaphoreType.DMA
    width = KEY_VALUE_HEADS * HEAD_SIZE
    dq, dk, dv, factor = pl.pallas_call(
        kernel,
        out_shape=(
            jax.ShapeDtypeStruct((TOK, QUERY_HEADS * HEAD_SIZE), bf16),
            jax.ShapeDtypeStruct((TOK, width), f32),
            jax.ShapeDtypeStruct((TOK, width), f32),
            jax.ShapeDtypeStruct((8, 128), f32),
        ),
        in_specs=[pl.BlockSpec(memory_space=pl.ANY)] * 5,
        out_specs=[pl.BlockSpec(memory_space=pl.ANY)] + [pl.BlockSpec(memory_space=vmem)] * 3,
        scratch_shapes=[
            vmem((ROWS, HALF_Q), bf16),
            vmem((ROWS, HALF_Q), bf16),
            vmem((2, SEQ, HEAD_SIZE), bf16),
            vmem((N_SP, 1, TOK), jnp.int32),
            vmem((ROWS, HALF_Q), bf16),
            vmem((SEQ, ALL), bf16),
            vmem((SEQ, ALL), bf16),
            vmem((8, ALL), f32),
            vmem((8, ALL), f32),
            vmem((HEAD_SIZE, ALL), f32),
            vmem((HEAD_SIZE, SEQ), bf16),
            vmem((2, SEQ, 2 * HEAD_SIZE), bf16),
            vmem((ROWS, HEAD_SIZE), bf16),
            vmem((2, SEQ, HEAD_SIZE), bf16),
            vmem((2, SEQ, HEAD_SIZE), bf16),
            vmem((TOK, HALF_Q), bf16),
            vmem((N_SP, 2, TOK, HEAD_SIZE), bf16),
            vmem((N_SP, 2, TOK, HEAD_SIZE), bf16),
            vmem((2, 8, 128), f32),
            vmem((N_SP, 8, 128), f32),
            vmem((N_GRP, 8, 128), f32),
            sems((5, 2)),
            sems((2, 2)),
            sems((2, 2)),
            sems((3, 2, N_SP)),
            sems((3, 2, N_SP)),
            sems((2, 2, N_SP)),
            sems((2, 2, N_SP)),
            sems((2,)),
            sems((2,)),
            sems((N_SP,)),
            sems((N_SP,)),
            sems((N_GRP,)),
            sems((N_GRP,)),
        ],
        compiler_params=pltpu.CompilerParams(
            collective_id=0, has_side_effects=True, vmem_limit_bytes=58 << 20
        ),
        name="attention_grads",
    )(query, grad_out, key, value, segment_ids.reshape(1, TOK))
    return scale(dq, dk, dv, factor)


def solution(mesh):
    whole = P(("grp", "sp"), None)
    return jax.shard_map(
        on_device,
        mesh=mesh,
        in_specs=(whole, whole, whole, whole, P(("grp", "sp"))),
        out_specs=(whole, whole, whole),
        check_vma=False,
    )
```

```python
import functools

import jax
import jax.numpy as jnp
from jax import lax
from jax.experimental import pallas as pl
from jax.experimental.pallas import tpu as pltpu
from jax.sharding import PartitionSpec as P

QUERY_HEADS = 48
KEY_VALUE_HEADS = 4
HEAD_SIZE = 128
TOK = 128
N_SP = 16
N_GRP = 16
ROWS = 2 * TOK
SEQ = TOK * N_SP
HALF_Q = QUERY_HEADS * HEAD_SIZE // 2
HALF_KV = KEY_VALUE_HEADS * HEAD_SIZE // 2
CORE_HEADS = QUERY_HEADS // 2
GROUP_HEADS = QUERY_HEADS // KEY_VALUE_HEADS
SCALE = HEAD_SIZE**-0.5
EXP2_SCALE = SCALE * 1.4426950408889634
NEG = -1e30
HB = 4
GROUPS = GROUP_HEADS // HB
ROW_KEYS = 4 * TOK
STEPS = 8
WIDE = HB * ROWS
ALL = GROUP_HEADS * ROWS
ITEMS = float(TOK * N_SP * N_GRP * (QUERY_HEADS + 2 * KEY_VALUE_HEADS) * HEAD_SIZE)

f32 = jnp.float32
bf16 = jnp.bfloat16
MESH = pl.DeviceIdType.MESH


def greet(axis, me, count):
    barrier = pltpu.get_barrier_semaphore()

    def one(d, z):
        other = lax.rem(me + d, count)
        pl.semaphore_signal(barrier, inc=1, device_id={axis: other}, device_id_type=MESH)
        return z

    lax.fori_loop(1, count, one, 0)


def span(index, size):
    return pl.ds(pl.multiple_of(index * size, size), size)


def nt(a, b):
    return lax.dot_general(a, b, (((1,), (1,)), ((), ())), preferred_element_type=f32)


def nn(a, b):
    return lax.dot_general(a, b, (((1,), (0,)), ((), ())), preferred_element_type=f32)


def columns(h, j):
    return span(h * GROUP_HEADS + j, HEAD_SIZE)


def ids_of(seg, index):
    return jnp.broadcast_to(seg[index].astype(f32), (TOK, TOK)).T


def prepare(h, row, seg, kt, kaug):
    for n in range(4):
        part = span(4 * row + n, TOK)
        kt[:, part] = kaug[h, part, 0:HEAD_SIZE].T

    @pl.when(h == 0)
    def _():
        lane = lax.broadcasted_iota(jnp.int32, (TOK, TOK), 1).astype(f32)
        for n in range(4):
            mask = jnp.where(ids_of(seg, 4 * row + n) == lane, 0.0, NEG).astype(bf16)
            for both in range(2):
                kaug[both, span(4 * row + n, TOK), HEAD_SIZE:] = mask


def scores(h, row, chip, diagonal, q, do, v, kaug, qoh, s_s, e_s, dp_s, top_s, stat_s):
    part = span(row, ROW_KEYS)
    tops = []
    for t in range(GROUPS):
        wide = slice(t * WIDE, (t + 1) * WIDE)
        qt = jnp.concatenate([q[:, columns(h, t * HB + j)] for j in range(HB)], axis=0)
        qa = jnp.concatenate([qt, jnp.concatenate([qoh[...]] * HB, axis=0)], axis=1)
        s = nt(kaug[h, part, :], qa)
        if diagonal:
            place = lax.broadcasted_iota(jnp.int32, (ROW_KEYS, WIDE), 0) + row * ROW_KEYS
            token = lax.broadcasted_iota(jnp.int32, (1, ROWS), 1) + chip * ROWS
            s = jnp.where(place <= jnp.concatenate([token] * HB, axis=1), s, NEG)
        s_s[:, wide] = s
        high = jnp.max(s, axis=0, keepdims=True)
        tops.append(high if diagonal else jnp.maximum(stat_s[0:1, wide], high))
    for t, high in enumerate(tops):
        wide = slice(t * WIDE, (t + 1) * WIDE)
        dt = jnp.concatenate([do[:, columns(h, t * HB + j)] for j in range(HB)], axis=0)
        dp = nt(v[h, part, :], dt)
        e = jnp.exp2((s_s[:, wide] - high) * EXP2_SCALE)
        total = jnp.sum(e, axis=0, keepdims=True)
        delta = jnp.sum(e * dp, axis=0, keepdims=True)
        if not diagonal:
            fade = jnp.exp2((stat_s[0:1, wide] - high) * EXP2_SCALE)
            total += stat_s[1:2, wide] * fade
            delta += stat_s[2:3, wide] * fade
        e_s[part, wide] = e.astype(bf16)
        dp_s[part, wide] = dp.astype(bf16)
        top_s[pl.ds(row, 1), wide] = high
        stat_s[0:1, wide] = high
        stat_s[1:2, wide] = total
        stat_s[2:3, wide] = delta


def grads(h, row, q, do, kt, e_s, dp_s, top_s, stat_s, dqt_s, dk_out, dv_out):
    qt = jnp.concatenate([q[:, columns(h, j)] for j in range(GROUP_HEADS)], axis=0)
    dt = jnp.concatenate([do[:, columns(h, j)] for j in range(GROUP_HEADS)], axis=0)
    inverse = 1.0 / stat_s[1:2, :]
    delta = (stat_s[2:3, :] * inverse).astype(bf16)
    part = span(row, ROW_KEYS)
    weight = jnp.exp2((top_s[pl.ds(row, 1), :] - stat_s[0:1, :]) * EXP2_SCALE) * inverse
    p = e_s[part, :] * weight.astype(bf16)
    ds = p * (dp_s[part, :] - delta)
    dv_out[h, part, :] = nn(p, dt).astype(bf16)
    dk_out[h, part, :] = (nn(ds, qt) * SCALE).astype(bf16)
    dqt_s[...] += nn(kt[:, part], ds)


def kernel(
    q, do, k, v, seg, dq_out, k_sum, v_sum, factor,
    q2, do2, v2, seg2, dq2, s_s, e_s, dp_s, top_s, stat_s, dqt_s, kt, kaug, qoh, dk_out, dv_out,
    dq_in, dk_in, dv_in, sq_mine, sq_sp, sq_grp,
    here, near_send, near_recv, far_send, far_recv, back_send, back_recv, dq_send, dq_recv,
    sp_send, sp_recv, grp_send, grp_recv,
):
    me = lax.axis_index("sp")
    group = lax.axis_index("grp")
    core = lax.rem(me, 2)
    chip = me // 2
    row = me // 4
    peer = me + 1 - 2 * core

    def remote(src, dst, send, recv, target):
        return pltpu.make_async_remote_copy(
            src_ref=src, dst_ref=dst, send_sem=send, recv_sem=recv, device_id={"sp": target}, device_id_type=MESH
        )

    def near(h):
        lanes = span((1 - core) * 2 + h, HALF_Q // 2)
        to = span(h, HALF_Q // 2)
        return [
            remote(a.at[:, lanes], b.at[span(core, TOK), to], near_send.at[n, h], near_recv.at[n, h], peer)
            for n, (a, b) in enumerate(((q, q2), (do, do2)))
        ]

    def far(h, src, target):
        lanes = span(lax.rem(target, 2) * 2 + h, HEAD_SIZE)
        part = span(src, TOK)
        return [
            remote(a.at[:, lanes], b, far_send.at[n, h, target], far_recv.at[n, h, src], target)
            for n, (a, b) in enumerate(((k, kaug.at[h, part, 0:HEAD_SIZE]), (v, v2.at[h, part, :])))
        ]

    def ids(src, target):
        return remote(seg, seg2.at[src], far_send.at[2, 0, target], far_recv.at[2, 0, src], target)

    def back(h, src, target):
        part = span(target, TOK)
        return [
            remote(a.at[h, part, :], b.at[src, h], back_send.at[n, h, target], back_recv.at[n, h, src], target)
            for n, (a, b) in enumerate(((dk_out, dk_in), (dv_out, dv_in)))
        ]

    def back_near(h):
        lanes = span(h, HALF_Q // 2)
        return remote(dq2.at[span(1 - core, TOK), lanes], dq_in.at[:, lanes], dq_send.at[h], dq_recv.at[h], peer)

    greet("sp", me, N_SP)
    greet("grp", group, N_GRP)
    def local(h):
        half = span(core * 2 + h, HALF_Q // 2)
        to = span(h, HALF_Q // 2)
        lanes = span(core * 2 + h, HEAD_SIZE)
        return [
            pltpu.make_async_copy(q.at[:, half], q2.at[span(core, TOK), to], here.at[0, h]),
            pltpu.make_async_copy(do.at[:, half], do2.at[span(core, TOK), to], here.at[1, h]),
            pltpu.make_async_copy(k.at[:, lanes], kaug.at[h, span(me, TOK), 0:HEAD_SIZE], here.at[2, h]),
            pltpu.make_async_copy(v.at[:, lanes], v2.at[h, span(me, TOK), :], here.at[3, h]),
        ]

    own_ids = pltpu.make_async_copy(seg, seg2.at[me], here.at[4, 0])
    own_ids.start()
    pl.semaphore_wait(pltpu.get_barrier_semaphore(), N_SP + N_GRP - 2)

    def send_all(h, z):
        for copy in near(h):
            copy.start()
        for copy in local(h):
            copy.start()

        def send(d, z):
            target = lax.rem(me + d, N_SP)

            @pl.when(target // 4 >= row)
            def _():
                for copy in far(h, me, target):
                    copy.start()

                @pl.when(h == 0)
                def _():
                    ids(me, target).start()

            return z

        return lax.fori_loop(1, N_SP, send, z)

    lax.fori_loop(0, 2, send_all, 0)
    own_ids.wait()
    lane = lax.broadcasted_iota(jnp.int32, (TOK, TOK), 1).astype(f32)

    def head(h, z):
        for copy in local(h):
            copy.wait()
        for copy in near(h):
            copy.wait_recv()

        def arrive(at):
            def one(n, z):
                other = 4 * at + n

                @pl.when(other != me)
                def _():
                    for copy in far(h, other, me):
                        copy.wait_recv()

                    @pl.when(h == 0)
                    def _():
                        ids(other, me).wait_recv()

                return z

            lax.fori_loop(0, 4, one, 0)
            prepare(h, at, seg2, kt, kaug)

        arrive(row)

        @pl.when(h == 0)
        def _():
            for c in range(2):
                hot = jnp.where(ids_of(seg2, 2 * chip + c) == lane, 1.0, 0.0)
                qoh[c * TOK : (c + 1) * TOK, :] = hot.astype(bf16)

        common = (q2, do2, v2, kaug, qoh, s_s, e_s, dp_s, top_s, stat_s)
        scores(h, row, chip, True, *common)

        def earlier(d, z):
            arrive(row - d)
            scores(h, row - d, chip, False, *common)
            return z

        lax.fori_loop(1, row + 1, earlier, 0)
        dqt_s[...] = jnp.zeros_like(dqt_s)

        def backward(at, z):
            grads(h, at, q2, do2, kt, e_s, dp_s, top_s, stat_s, dqt_s, dk_out, dv_out)

            def give(n, z):
                target = 4 * at + n

                @pl.when((target // 2 <= chip) & (target != me))
                def _():
                    for copy in back(h, me, target):
                        copy.start()

                return z

            return lax.fori_loop(0, 4, give, z)

        lax.fori_loop(0, row + 1, backward, 0)
        for j in range(GROUP_HEADS):
            out = dqt_s[:, j * ROWS : (j + 1) * ROWS] * SCALE
            dq2[:, columns(h, j)] = out.astype(bf16).T
        back_near(h).start()
        return z

    lax.fori_loop(0, 2, head, 0)

    def square(x):
        x = x.astype(f32)
        return jnp.sum(x * x)

    own = dq2.at[span(core, TOK), :]
    out = [
        pltpu.make_async_copy(own, dq_out.at[:, span(core, HALF_Q)], here.at[0, 0]),
        pltpu.make_async_copy(dq_in, dq_out.at[:, span(1 - core, HALF_Q)], here.at[1, 0]),
    ]
    out[0].start()
    squares = square(own[...])

    def halves(g, z):
        back_near(g).wait()
        return z

    lax.fori_loop(0, 2, halves, 0)
    out[1].start()
    squares += square(dq_in[...])
    for c in range(2):
        for h in range(2):
            lanes = slice((2 * c + h) * HEAD_SIZE, (2 * c + h + 1) * HEAD_SIZE)
            k_sum[:, lanes] = jnp.zeros((TOK, HEAD_SIZE), f32)
            v_sum[:, lanes] = jnp.zeros((TOK, HEAD_SIZE), f32)

            @pl.when(core == c)
            def _():
                k_sum[:, lanes] = dk_out[h, span(me, TOK), :].astype(f32)
                v_sum[:, lanes] = dv_out[h, span(me, TOK), :].astype(f32)

    for h in range(2):

        def add(j, z):
            for c in range(2):
                other = 2 * j + c

                @pl.when(other != me)
                def _():
                    for copy in back(h, other, me):
                        copy.wait_recv()
                    lanes = slice((2 * c + h) * HEAD_SIZE, (2 * c + h + 1) * HEAD_SIZE)
                    k_sum[:, lanes] += dk_in[other, h].astype(f32)
                    v_sum[:, lanes] += dv_in[other, h].astype(f32)

            return z

        lax.fori_loop(chip, N_SP // 2, add, 0)
    squares += square(k_sum[...]) + square(v_sum[...])

    def settle():
        def one(d, z):
            other = lax.rem(me + d, N_SP)

            @pl.when(other // 4 >= row)
            def _():
                for h in range(2):
                    for copy in far(h, me, other):
                        copy.wait_send()
                ids(me, other).wait_send()

            @pl.when(other // 2 <= chip)
            def _():
                for h in range(2):
                    for copy in back(h, me, other):
                        copy.wait_send()

            return z

        lax.fori_loop(1, N_SP, one, 0)
        for h in range(2):
            for copy in near(h):
                copy.wait_send()
        for copy in out:
            copy.wait()

    def share(stage, axis, index, count, slots, sends, recvs, amount, beside):
        sq_mine[stage] = jnp.full((8, 128), amount, f32)

        def message(src, target):
            return pltpu.make_async_remote_copy(
                src_ref=sq_mine.at[stage],
                dst_ref=slots.at[src],
                send_sem=sends.at[target],
                recv_sem=recvs.at[src],
                device_id={axis: target},
                device_id_type=MESH,
            )

        for d in range(1, count):
            message(index, lax.rem(index + d, count)).start()
        slots[index] = sq_mine[stage]
        beside()
        for d in range(1, count):
            message(lax.rem(index + d, count), index).wait_recv()

        def sent():
            for d in range(1, count):
                message(index, lax.rem(index + d, count)).wait_send()

        return jnp.max(jnp.sum(slots[...], axis=0)), sent

    squares, sent_sp = share(0, "sp", me, N_SP, sq_sp, sp_send, sp_recv, squares, settle)
    squares, sent_grp = share(1, "grp", group, N_GRP, sq_grp, grp_send, grp_recv, squares, sent_sp)
    sent_grp()
    factor[...] = 1.0 / jnp.sqrt(jnp.full((8, 128), squares, f32) / ITEMS + 1e-6)


def scale_kernel(dq, dk, dv, factor, gq, gk, gv, x, xk, xv, by, y, yk, yv, come, go):
    rows = TOK // STEPS
    parts = [slice(i * rows, (i + 1) * rows) for i in range(STEPS)]
    moves = [(dk, xk, yk, gk), (dv, xv, yv, gv)]
    moves += [(dq.at[p, :], x.at[p, :], y.at[p, :], gq.at[p, :]) for p in parts]
    head = pltpu.make_async_copy(factor, by, come.at[STEPS + 2])
    head.start()
    enter = [pltpu.make_async_copy(m[0], m[1], come.at[i]) for i, m in enumerate(moves)]
    leave = [pltpu.make_async_copy(m[2], m[3], go.at[i]) for i, m in enumerate(moves)]
    for copy in enter:
        copy.start()
    head.wait()
    value = by[0:1, 0:1]
    for i, m in enumerate(moves):
        enter[i].wait()
        m[2][...] = (m[1][...].astype(f32) * value).astype(bf16)
        leave[i].start()
    for copy in leave:
        copy.wait()


def scale(dq, dk, dv, factor):
    far = pl.BlockSpec(memory_space=pl.ANY)
    vmem = pltpu.VMEM
    return pl.pallas_call(
        scale_kernel,
        out_shape=tuple(jax.ShapeDtypeStruct(x.shape, bf16) for x in (dq, dk, dv)),
        in_specs=[far] * 4,
        out_specs=[far] * 3,
        scratch_shapes=[
            vmem(dq.shape, bf16),
            vmem(dk.shape, f32),
            vmem(dv.shape, f32),
            vmem(factor.shape, f32),
            vmem(dq.shape, bf16),
            vmem(dk.shape, bf16),
            vmem(dv.shape, bf16),
            pltpu.SemaphoreType.DMA((STEPS + 3,)),
            pltpu.SemaphoreType.DMA((STEPS + 2,)),
        ],
        name="scale",
    )(dq, dk, dv, factor)


def on_device(query, key, value, grad_out, segment_ids):
    vmem = pltpu.VMEM
    sems = pltpu.SemaphoreType.DMA
    width = KEY_VALUE_HEADS * HEAD_SIZE
    dq, dk, dv, factor = pl.pallas_call(
        kernel,
        out_shape=(
            jax.ShapeDtypeStruct((TOK, QUERY_HEADS * HEAD_SIZE), bf16),
            jax.ShapeDtypeStruct((TOK, width), f32),
            jax.ShapeDtypeStruct((TOK, width), f32),
            jax.ShapeDtypeStruct((8, 128), f32),
        ),
        in_specs=[pl.BlockSpec(memory_space=pl.ANY)] * 5,
        out_specs=[pl.BlockSpec(memory_space=pl.ANY)] + [pl.BlockSpec(memory_space=vmem)] * 3,
        scratch_shapes=[
            vmem((ROWS, HALF_Q), bf16),
            vmem((ROWS, HALF_Q), bf16),
            vmem((2, SEQ, HEAD_SIZE), bf16),
            vmem((N_SP, 1, TOK), jnp.int32),
            vmem((ROWS, HALF_Q), bf16),
            vmem((ROW_KEYS, ALL), f32),
            vmem((SEQ, ALL), bf16),
            vmem((SEQ, ALL), bf16),
            vmem((8, ALL), f32),
            vmem((8, ALL), f32),
            vmem((HEAD_SIZE, ALL), f32),
            vmem((HEAD_SIZE, SEQ), bf16),
            vmem((2, SEQ, 2 * HEAD_SIZE), bf16),
            vmem((ROWS, HEAD_SIZE), bf16),
            vmem((2, SEQ, HEAD_SIZE), bf16),
            vmem((2, SEQ, HEAD_SIZE), bf16),
            vmem((TOK, HALF_Q), bf16),
            vmem((N_SP, 2, TOK, HEAD_SIZE), bf16),
            vmem((N_SP, 2, TOK, HEAD_SIZE), bf16),
            vmem((2, 8, 128), f32),
            vmem((N_SP, 8, 128), f32),
            vmem((N_GRP, 8, 128), f32),
            sems((5, 2)),
            sems((2, 2)),
            sems((2, 2)),
            sems((3, 2, N_SP)),
            sems((3, 2, N_SP)),
            sems((2, 2, N_SP)),
            sems((2, 2, N_SP)),
            sems((2,)),
            sems((2,)),
            sems((N_SP,)),
            sems((N_SP,)),
            sems((N_GRP,)),
            sems((N_GRP,)),
        ],
        compiler_params=pltpu.CompilerParams(
            collective_id=0, has_side_effects=True, vmem_limit_bytes=58 << 20
        ),
        name="attention_grads",
    )(query, grad_out, key, value, segment_ids.reshape(1, TOK))
    return scale(dq, dk, dv, factor)


def solution(mesh):
    whole = P(("grp", "sp"), None)
    return jax.shard_map(
        on_device,
        mesh=mesh,
        in_specs=(whole, whole, whole, whole, P(("grp", "sp"))),
        out_specs=(whole, whole, whole),
        check_vma=False,
    )
```

```python
import functools

import jax
import jax.numpy as jnp
from jax import lax
from jax.experimental import pallas as pl
from jax.experimental.pallas import tpu as pltpu
from jax.sharding import PartitionSpec as P

QUERY_HEADS = 48
KEY_VALUE_HEADS = 4
HEAD_SIZE = 128
TOK = 128
N_SP = 16
N_GRP = 16
ROWS = 2 * TOK
SEQ = TOK * N_SP
HALF_Q = QUERY_HEADS * HEAD_SIZE // 2
HALF_KV = KEY_VALUE_HEADS * HEAD_SIZE // 2
CORE_HEADS = QUERY_HEADS // 2
GROUP_HEADS = QUERY_HEADS // KEY_VALUE_HEADS
SCALE = HEAD_SIZE**-0.5
EXP2_SCALE = SCALE * 1.4426950408889634
NEG = -1e30
HB = 4
GROUPS = GROUP_HEADS // HB
ROW_KEYS = 4 * TOK
STEPS = 8
WIDE = HB * ROWS
ALL = GROUP_HEADS * ROWS
ITEMS = float(TOK * N_SP * N_GRP * (QUERY_HEADS + 2 * KEY_VALUE_HEADS) * HEAD_SIZE)

f32 = jnp.float32
bf16 = jnp.bfloat16
MESH = pl.DeviceIdType.MESH


def greet(axis, me, count):
    barrier = pltpu.get_barrier_semaphore()

    def one(d, z):
        other = lax.rem(me + d, count)
        pl.semaphore_signal(barrier, inc=1, device_id={axis: other}, device_id_type=MESH)
        return z

    lax.fori_loop(1, count, one, 0)


def span(index, size):
    return pl.ds(pl.multiple_of(index * size, size), size)


def nt(a, b):
    return lax.dot_general(a, b, (((1,), (1,)), ((), ())), preferred_element_type=f32)


def nn(a, b):
    return lax.dot_general(a, b, (((1,), (0,)), ((), ())), preferred_element_type=f32)


def columns(h, j):
    return span(h * GROUP_HEADS + j, HEAD_SIZE)


def ids_of(seg, index):
    return jnp.broadcast_to(seg[index].astype(f32), (TOK, TOK)).T


def prepare(h, row, seg, kt, kaug):
    for n in range(4):
        part = span(4 * row + n, TOK)
        kt[:, part] = kaug[h, part, 0:HEAD_SIZE].T

    @pl.when(h == 0)
    def _():
        lane = lax.broadcasted_iota(jnp.int32, (TOK, TOK), 1).astype(f32)
        for n in range(4):
            mask = jnp.where(ids_of(seg, 4 * row + n) == lane, 0.0, NEG).astype(bf16)
            for both in range(2):
                kaug[both, span(4 * row + n, TOK), HEAD_SIZE:] = mask


def scores(h, row, chip, diagonal, q, do, v, kaug, qoh, s_s, e_s, dp_s, top_s, stat_s):
    part = span(row, ROW_KEYS)
    tops = []
    for t in range(GROUPS):
        wide = slice(t * WIDE, (t + 1) * WIDE)
        qt = jnp.concatenate([q[:, columns(h, t * HB + j)] for j in range(HB)], axis=0)
        qa = jnp.concatenate([qt, jnp.concatenate([qoh[...]] * HB, axis=0)], axis=1)
        s = nt(kaug[h, part, :], qa)
        if diagonal:
            place = lax.broadcasted_iota(jnp.int32, (ROW_KEYS, WIDE), 0) + row * ROW_KEYS
            token = lax.broadcasted_iota(jnp.int32, (1, ROWS), 1) + chip * ROWS
            s = jnp.where(place <= jnp.concatenate([token] * HB, axis=1), s, NEG)
        s_s[:, wide] = s
        high = jnp.max(s, axis=0, keepdims=True)
        tops.append(high if diagonal else jnp.maximum(stat_s[0:1, wide], high))
    for t, high in enumerate(tops):
        wide = slice(t * WIDE, (t + 1) * WIDE)
        dt = jnp.concatenate([do[:, columns(h, t * HB + j)] for j in range(HB)], axis=0)
        dp = nt(v[h, part, :], dt)
        e = jnp.exp2((s_s[:, wide] - high) * EXP2_SCALE)
        total = jnp.sum(e, axis=0, keepdims=True)
        delta = jnp.sum(e * dp, axis=0, keepdims=True)
        if not diagonal:
            fade = jnp.exp2((stat_s[0:1, wide] - high) * EXP2_SCALE)
            total += stat_s[1:2, wide] * fade
            delta += stat_s[2:3, wide] * fade
        e_s[part, wide] = e.astype(bf16)
        dp_s[part, wide] = dp.astype(bf16)
        top_s[pl.ds(row, 1), wide] = high
        stat_s[0:1, wide] = high
        stat_s[1:2, wide] = total
        stat_s[2:3, wide] = delta


def grads(h, row, q, do, kt, e_s, dp_s, top_s, stat_s, dqt_s, dk_out, dv_out):
    qt = jnp.concatenate([q[:, columns(h, j)] for j in range(GROUP_HEADS)], axis=0)
    dt = jnp.concatenate([do[:, columns(h, j)] for j in range(GROUP_HEADS)], axis=0)
    inverse = 1.0 / stat_s[1:2, :]
    delta = (stat_s[2:3, :] * inverse).astype(bf16)
    part = span(row, ROW_KEYS)
    weight = jnp.exp2((top_s[pl.ds(row, 1), :] - stat_s[0:1, :]) * EXP2_SCALE) * inverse
    p = e_s[part, :] * weight.astype(bf16)
    ds = p * (dp_s[part, :] - delta)
    dv_out[h, part, :] = nn(p, dt).astype(bf16)
    dk_out[h, part, :] = (nn(ds, qt) * SCALE).astype(bf16)
    dqt_s[...] += nn(kt[:, part], ds)


def kernel(
    q, do, k, v, seg, dq_out, k_sum, v_sum, factor,
    q2, do2, v2, seg2, dq2, s_s, e_s, dp_s, top_s, stat_s, dqt_s, kt, kaug, qoh, dk_out, dv_out,
    dq_in, dk_in, dv_in, sq_mine, sq_sp, sq_grp,
    here, near_send, near_recv, far_send, far_recv, back_send, back_recv, dq_send, dq_recv,
    sp_send, sp_recv, grp_send, grp_recv,
):
    me = lax.axis_index("sp")
    group = lax.axis_index("grp")
    core = lax.rem(me, 2)
    chip = me // 2
    row = me // 4
    peer = me + 1 - 2 * core

    def remote(src, dst, send, recv, target):
        return pltpu.make_async_remote_copy(
            src_ref=src, dst_ref=dst, send_sem=send, recv_sem=recv, device_id={"sp": target}, device_id_type=MESH
        )

    def near(h):
        lanes = span((1 - core) * 2 + h, HALF_Q // 2)
        to = span(h, HALF_Q // 2)
        return [
            remote(a.at[:, lanes], b.at[span(core, TOK), to], near_send.at[n, h], near_recv.at[n, h], peer)
            for n, (a, b) in enumerate(((q, q2), (do, do2)))
        ]

    def far(h, src, target):
        lanes = span(lax.rem(target, 2) * 2 + h, HEAD_SIZE)
        part = span(src, TOK)
        return [
            remote(a.at[:, lanes], b, far_send.at[n, h, target], far_recv.at[n, h, src], target)
            for n, (a, b) in enumerate(((k, kaug.at[h, part, 0:HEAD_SIZE]), (v, v2.at[h, part, :])))
        ]

    def ids(src, target):
        return remote(seg, seg2.at[src], far_send.at[2, 0, target], far_recv.at[2, 0, src], target)

    def back(h, src, target):
        part = span(target, TOK)
        return [
            remote(a.at[h, part, :], b.at[src, h], back_send.at[n, h, target], back_recv.at[n, h, src], target)
            for n, (a, b) in enumerate(((dk_out, dk_in), (dv_out, dv_in)))
        ]

    def back_near(h):
        lanes = span(h, HALF_Q // 2)
        return remote(dq2.at[span(1 - core, TOK), lanes], dq_in.at[:, lanes], dq_send.at[h], dq_recv.at[h], peer)

    greet("sp", me, N_SP)
    greet("grp", group, N_GRP)
    def local(h):
        half = span(core * 2 + h, HALF_Q // 2)
        to = span(h, HALF_Q // 2)
        lanes = span(core * 2 + h, HEAD_SIZE)
        return [
            pltpu.make_async_copy(q.at[:, half], q2.at[span(core, TOK), to], here.at[0, h]),
            pltpu.make_async_copy(do.at[:, half], do2.at[span(core, TOK), to], here.at[1, h]),
            pltpu.make_async_copy(k.at[:, lanes], kaug.at[h, span(me, TOK), 0:HEAD_SIZE], here.at[2, h]),
            pltpu.make_async_copy(v.at[:, lanes], v2.at[h, span(me, TOK), :], here.at[3, h]),
        ]

    own_ids = pltpu.make_async_copy(seg, seg2.at[me], here.at[4, 0])
    own_ids.start()
    pl.semaphore_wait(pltpu.get_barrier_semaphore(), N_SP + N_GRP - 2)

    def send_all(h, z):
        for copy in near(h):
            copy.start()
        for copy in local(h):
            copy.start()

        def send(d, z):
            target = lax.rem(me + d, N_SP)

            @pl.when(target // 4 >= row)
            def _():
                for copy in far(h, me, target):
                    copy.start()

                @pl.when(h == 0)
                def _():
                    ids(me, target).start()

            return z

        return lax.fori_loop(1, N_SP, send, z)

    lax.fori_loop(0, 2, send_all, 0)
    own_ids.wait()
    lane = lax.broadcasted_iota(jnp.int32, (TOK, TOK), 1).astype(f32)

    def head(h, z):
        for copy in local(h):
            copy.wait()
        for copy in near(h):
            copy.wait_recv()

        def arrive(at):
            def one(n, z):
                other = 4 * at + n

                @pl.when(other != me)
                def _():
                    for copy in far(h, other, me):
                        copy.wait_recv()

                    @pl.when(h == 0)
                    def _():
                        ids(other, me).wait_recv()

                return z

            lax.fori_loop(0, 4, one, 0)
            prepare(h, at, seg2, kt, kaug)

        arrive(row)

        @pl.when(h == 0)
        def _():
            for c in range(2):
                hot = jnp.where(ids_of(seg2, 2 * chip + c) == lane, 1.0, 0.0)
                qoh[c * TOK : (c + 1) * TOK, :] = hot.astype(bf16)

        common = (q2, do2, v2, kaug, qoh, s_s, e_s, dp_s, top_s, stat_s)
        scores(h, row, chip, True, *common)

        def earlier(d, z):
            arrive(row - d)
            scores(h, row - d, chip, False, *common)
            return z

        lax.fori_loop(1, row + 1, earlier, 0)
        dqt_s[...] = jnp.zeros_like(dqt_s)

        def backward(step, z):
            at = lax.rem(step + 1, row + 1)
            grads(h, at, q2, do2, kt, e_s, dp_s, top_s, stat_s, dqt_s, dk_out, dv_out)

            def give(n, z):
                target = 4 * at + n

                @pl.when((target // 2 <= chip) & (target != me))
                def _():
                    for copy in back(h, me, target):
                        copy.start()

                return z

            return lax.fori_loop(0, 4, give, z)

        lax.fori_loop(0, row + 1, backward, 0)
        for j in range(GROUP_HEADS):
            out = dqt_s[:, j * ROWS : (j + 1) * ROWS] * SCALE
            dq2[:, columns(h, j)] = out.astype(bf16).T
        back_near(h).start()
        return z

    lax.fori_loop(0, 2, head, 0)

    def square(x):
        x = x.astype(f32)
        return jnp.sum(x * x)

    own = dq2.at[span(core, TOK), :]
    out = [
        pltpu.make_async_copy(own, dq_out.at[:, span(core, HALF_Q)], here.at[0, 0]),
        pltpu.make_async_copy(dq_in, dq_out.at[:, span(1 - core, HALF_Q)], here.at[1, 0]),
    ]
    out[0].start()
    squares = square(own[...])

    def halves(g, z):
        back_near(g).wait()
        return z

    lax.fori_loop(0, 2, halves, 0)
    out[1].start()
    squares += square(dq_in[...])
    for c in range(2):
        for h in range(2):
            lanes = slice((2 * c + h) * HEAD_SIZE, (2 * c + h + 1) * HEAD_SIZE)
            k_sum[:, lanes] = jnp.zeros((TOK, HEAD_SIZE), f32)
            v_sum[:, lanes] = jnp.zeros((TOK, HEAD_SIZE), f32)

            @pl.when(core == c)
            def _():
                k_sum[:, lanes] = dk_out[h, span(me, TOK), :].astype(f32)
                v_sum[:, lanes] = dv_out[h, span(me, TOK), :].astype(f32)

    for h in range(2):

        def add(j, z):
            for c in range(2):
                other = 2 * j + c

                @pl.when(other != me)
                def _():
                    for copy in back(h, other, me):
                        copy.wait_recv()
                    lanes = slice((2 * c + h) * HEAD_SIZE, (2 * c + h + 1) * HEAD_SIZE)
                    k_sum[:, lanes] += dk_in[other, h].astype(f32)
                    v_sum[:, lanes] += dv_in[other, h].astype(f32)

            return z

        lax.fori_loop(chip, N_SP // 2, add, 0)
    squares += square(k_sum[...]) + square(v_sum[...])

    def settle():
        def one(d, z):
            other = lax.rem(me + d, N_SP)

            @pl.when(other // 4 >= row)
            def _():
                for h in range(2):
                    for copy in far(h, me, other):
                        copy.wait_send()
                ids(me, other).wait_send()

            @pl.when(other // 2 <= chip)
            def _():
                for h in range(2):
                    for copy in back(h, me, other):
                        copy.wait_send()

            return z

        lax.fori_loop(1, N_SP, one, 0)
        for h in range(2):
            for copy in near(h):
                copy.wait_send()
        for copy in out:
            copy.wait()

    def share(stage, axis, index, count, slots, sends, recvs, amount, beside):
        sq_mine[stage] = jnp.full((8, 128), amount, f32)

        def message(src, target):
            return pltpu.make_async_remote_copy(
                src_ref=sq_mine.at[stage],
                dst_ref=slots.at[src],
                send_sem=sends.at[target],
                recv_sem=recvs.at[src],
                device_id={axis: target},
                device_id_type=MESH,
            )

        for d in range(1, count):
            message(index, lax.rem(index + d, count)).start()
        slots[index] = sq_mine[stage]
        beside()
        for d in range(1, count):
            message(lax.rem(index + d, count), index).wait_recv()

        def sent():
            for d in range(1, count):
                message(index, lax.rem(index + d, count)).wait_send()

        return jnp.max(jnp.sum(slots[...], axis=0)), sent

    squares, sent_sp = share(0, "sp", me, N_SP, sq_sp, sp_send, sp_recv, squares, settle)
    squares, sent_grp = share(1, "grp", group, N_GRP, sq_grp, grp_send, grp_recv, squares, sent_sp)
    sent_grp()
    factor[...] = 1.0 / jnp.sqrt(jnp.full((8, 128), squares, f32) / ITEMS + 1e-6)


def scale_kernel(dq, dk, dv, factor, gq, gk, gv, x, xk, xv, by, y, yk, yv, come, go):
    rows = TOK // STEPS
    parts = [slice(i * rows, (i + 1) * rows) for i in range(STEPS)]
    moves = [(dk, xk, yk, gk), (dv, xv, yv, gv)]
    moves += [(dq.at[p, :], x.at[p, :], y.at[p, :], gq.at[p, :]) for p in parts]
    head = pltpu.make_async_copy(factor, by, come.at[STEPS + 2])
    head.start()
    enter = [pltpu.make_async_copy(m[0], m[1], come.at[i]) for i, m in enumerate(moves)]
    leave = [pltpu.make_async_copy(m[2], m[3], go.at[i]) for i, m in enumerate(moves)]
    for copy in enter:
        copy.start()
    head.wait()
    value = by[0:1, 0:1]
    for i, m in enumerate(moves):
        enter[i].wait()
        m[2][...] = (m[1][...].astype(f32) * value).astype(bf16)
        leave[i].start()
    for copy in leave:
        copy.wait()


def scale(dq, dk, dv, factor):
    far = pl.BlockSpec(memory_space=pl.ANY)
    vmem = pltpu.VMEM
    return pl.pallas_call(
        scale_kernel,
        out_shape=tuple(jax.ShapeDtypeStruct(x.shape, bf16) for x in (dq, dk, dv)),
        in_specs=[far] * 4,
        out_specs=[far] * 3,
        scratch_shapes=[
            vmem(dq.shape, bf16),
            vmem(dk.shape, f32),
            vmem(dv.shape, f32),
            vmem(factor.shape, f32),
            vmem(dq.shape, bf16),
            vmem(dk.shape, bf16),
            vmem(dv.shape, bf16),
            pltpu.SemaphoreType.DMA((STEPS + 3,)),
            pltpu.SemaphoreType.DMA((STEPS + 2,)),
        ],
        name="scale",
    )(dq, dk, dv, factor)


def on_device(query, key, value, grad_out, segment_ids):
    vmem = pltpu.VMEM
    sems = pltpu.SemaphoreType.DMA
    width = KEY_VALUE_HEADS * HEAD_SIZE
    dq, dk, dv, factor = pl.pallas_call(
        kernel,
        out_shape=(
            jax.ShapeDtypeStruct((TOK, QUERY_HEADS * HEAD_SIZE), bf16),
            jax.ShapeDtypeStruct((TOK, width), f32),
            jax.ShapeDtypeStruct((TOK, width), f32),
            jax.ShapeDtypeStruct((8, 128), f32),
        ),
        in_specs=[pl.BlockSpec(memory_space=pl.ANY)] * 5,
        out_specs=[pl.BlockSpec(memory_space=pl.ANY)] + [pl.BlockSpec(memory_space=vmem)] * 3,
        scratch_shapes=[
            vmem((ROWS, HALF_Q), bf16),
            vmem((ROWS, HALF_Q), bf16),
            vmem((2, SEQ, HEAD_SIZE), bf16),
            vmem((N_SP, 1, TOK), jnp.int32),
            vmem((ROWS, HALF_Q), bf16),
            vmem((ROW_KEYS, ALL), f32),
            vmem((SEQ, ALL), bf16),
            vmem((SEQ, ALL), bf16),
            vmem((8, ALL), f32),
            vmem((8, ALL), f32),
            vmem((HEAD_SIZE, ALL), f32),
            vmem((HEAD_SIZE, SEQ), bf16),
            vmem((2, SEQ, 2 * HEAD_SIZE), bf16),
            vmem((ROWS, HEAD_SIZE), bf16),
            vmem((2, SEQ, HEAD_SIZE), bf16),
            vmem((2, SEQ, HEAD_SIZE), bf16),
            vmem((TOK, HALF_Q), bf16),
            vmem((N_SP, 2, TOK, HEAD_SIZE), bf16),
            vmem((N_SP, 2, TOK, HEAD_SIZE), bf16),
            vmem((2, 8, 128), f32),
            vmem((N_SP, 8, 128), f32),
            vmem((N_GRP, 8, 128), f32),
            sems((5, 2)),
            sems((2, 2)),
            sems((2, 2)),
            sems((3, 2, N_SP)),
            sems((3, 2, N_SP)),
            sems((2, 2, N_SP)),
            sems((2, 2, N_SP)),
            sems((2,)),
            sems((2,)),
            sems((N_SP,)),
            sems((N_SP,)),
            sems((N_GRP,)),
            sems((N_GRP,)),
        ],
        compiler_params=pltpu.CompilerParams(
            collective_id=0, has_side_effects=True, vmem_limit_bytes=58 << 20
        ),
        name="attention_grads",
    )(query, grad_out, key, value, segment_ids.reshape(1, TOK))
    return scale(dq, dk, dv, factor)


def solution(mesh):
    whole = P(("grp", "sp"), None)
    return jax.shard_map(
        on_device,
        mesh=mesh,
        in_specs=(whole, whole, whole, whole, P(("grp", "sp"))),
        out_specs=(whole, whole, whole),
        check_vma=False,
    )
```
